32 devices in a mesh: row: 4 (over y, core), col: 8 (over z, x).
Axes of the slice: x: 2, y: 2, z: 4, core: 2. Of those that a mesh axis runs over, the one named last changes fastest.
Arguments:
- atoms: bfloat16 [4096, 128], P(('row', 'col')), may hold values from -6 to 6
- atom_pair: bfloat16 [128, 16, 32, 128], P(('row', 'col')), may hold values from -6 to 6
- atom_token: int32 [4096], P(('row', 'col')), may hold values from 0 to 1023, as said below
- single: bfloat16 [1024, 768], P('row'), may hold values from -6 to 6
- pair: bfloat16 [1024, 1024, 128], P('row', 'col'), may hold values from -6 to 6
- atom_w: bfloat16 [128, 4, 128], replicated, may hold values from -0.5 to 0.5
- atom_pair_w: bfloat16 [16, 4], replicated, may hold values from -24 to 24
- atom_wo: bfloat16 [128, 128], replicated, may hold values from -0.5 to 0.5
- agg_w: bfloat16 [128, 768], replicated, may hold values from -0.5 to 0.5
- trans_in: bfloat16 [128, 2, 256], replicated, may hold values from -0.5 to 0.5
- trans_out: bfloat16 [256, 128], replicated, may hold values from -0.375 to 0.375
- bias_w: bfloat16 [128, 16], replicated, may hold values from -6 to 6
- token_w: bfloat16 [768, 4, 768], P(None, None, 'col'), may hold values from -0.21875 to 0.21875
- token_wo: bfloat16 [768, 768], P('col'), may hold values from -0.21875 to 0.21875
- back_w: bfloat16 [768, 128], P('col'), may hold values from -0.21875 to 0.21875
Outputs:
- single_out: bfloat16 [1024, 768], P('row', 'col')
- atoms_out: bfloat16 [4096, 128], P(('row', 'col'))
The draws below stay inside these ranges and needn't reach their ends.
Inputs may be any that keep to these rules, and one draw needn't show every extreme that they name: `atom_token`: atoms are in token order; the 1024 atoms of block b (b from 0) belong to tokens b * 256 to (b + 1) * 256 - 1; every token has 1 to 7 atoms, and in every block some token has exactly 7.
All inputs are finite; a program needn't handle non-finite values.
Results may differ from the reference program's by a relative error of at most 0.024.
The reference program's roundings to bfloat16 on the way count: a program that leaves them out, or rounds other values in their place, can miss the bound.
Values may be sent and summed in bfloat16 or wider, within the bound.
A program may use at most 64 MiB of HBM per device.

```python
import math
import jax
import jax.numpy as jnp
from jax import lax

D = 768
HEADS = 16
HEAD = 48
CZ = 128
FFZ = 256
CA = 128
ATOM_HEADS = 4
ATOM_HEAD = 32
CP = 16
QW = 32
KW = 128
W_DEV = 4
TOKENS = 1024
TQ = 256
WINDOWS = 128
ATOMS = 4096
N_ROW = 4
N_COL = 8


def draw_atom_token(key, part):
    key = jax.random.fold_in(key, 5)
    per_row = QW * W_DEV * N_COL
    average = per_row // TQ
    half_rows = TQ // 2
    shift_key, order_key = jax.random.split(key)
    shifts = jax.random.randint(shift_key, (N_ROW, half_rows), 1 - average, average)
    shifts = shifts.at[:, 0].set(average - 1)
    counts = jnp.concatenate([average + shifts, average - shifts], axis=1)
    orders = jax.vmap(lambda row_key: jax.random.permutation(row_key, TQ))(jax.random.split(order_key, N_ROW))
    counts = jnp.take_along_axis(counts, orders, axis=1)
    bounds = jnp.cumsum(counts, axis=1)
    positions = jnp.arange(per_row)
    within = jnp.sum((bounds[:, None, :] <= positions[None, :, None]).astype(jnp.int32), axis=2)
    owners = within + (jnp.arange(N_ROW) * TQ)[:, None]
    return owners.reshape(ATOMS).astype(jnp.int32)


def draw_atom_pair_w(key, part):
    key = jax.random.fold_in(key, 11)
    values = jnp.clip(jax.random.normal(key, (CP, ATOM_HEADS), jnp.float32) * 0.5, -24.0, 24.0)
    return values.astype(jnp.bfloat16)


def draw_bias_w(key, part):
    key = jax.random.fold_in(key, 17)
    values = jnp.clip(jax.random.normal(key, (CZ, HEADS), jnp.float32) * (1.5 / CZ ** 0.5), -6.0, 6.0)
    return values.astype(jnp.bfloat16)


def levels(key, shape, cuts, least, top_value):
    def one(dim, blocks):
        heights = jax.random.uniform(jax.random.fold_in(jax.random.fold_in(key, 6), dim), (blocks,), jnp.float32, least / len(cuts), top_value / len(cuts))
        return jnp.repeat(jnp.exp(heights), shape[dim] // blocks).reshape((-1,) + (1,) * (len(shape) - dim - 1))

    gain = one(*cuts[0])
    for cut in cuts[1:]:
        gain = gain * one(*cut)
    return gain


def gaussian(own_key, shape, deviation, bound, pieces=(), held_as=jnp.bfloat16):
    array = jax.random.normal(own_key, shape, jnp.float32) * deviation
    if len(pieces) > 0:
        array = levels(own_key, shape, pieces, -0.22, 0.18) * array
    return jnp.clip(array, min=-bound, max=bound).astype(held_as)


def setup_inputs(seed: int = 0) -> dict:
    key_list = jax.random.split(jax.random.key(seed), 16)
    return {
        "atoms": gaussian(key_list[0], (ATOMS, CA), 1.0, 6.0, ((0, 32),)),
        "atom_pair": gaussian(key_list[1], (WINDOWS, CP, QW, KW), 1.0, 6.0, ((0, 32),)),
        "atom_token": draw_atom_token(jax.random.fold_in(key_list[15], 71), 0),
        "single": gaussian(key_list[3], (TOKENS, D), 1.0, 6.0, ((0, 4),)),
        "pair": gaussian(key_list[4], (TOKENS, TOKENS, CZ), 1.0, 6.0, ((0, 4), (1, 8))),
        "atom_w": gaussian(key_list[5], (CA, 4, CA), CA ** -0.5, 0.5),
        "atom_pair_w": draw_atom_pair_w(jax.random.fold_in(key_list[15], 71), 0),
        "atom_wo": gaussian(key_list[7], (CA, CA), CA ** -0.5, 0.5),
        "agg_w": gaussian(key_list[8], (CA, D), CA ** -0.5, 0.5),
        "trans_in": gaussian(key_list[9], (CZ, 2, FFZ), CZ ** -0.5, 0.5),
        "trans_out": gaussian(key_list[10], (FFZ, CZ), FFZ ** -0.5, 0.375),
        "bias_w": draw_bias_w(jax.random.fold_in(key_list[15], 71), 0),
        "token_w": gaussian(key_list[12], (D, 4, D), D ** -0.5, 0.21875, ((2, 8),)),
        "token_wo": gaussian(key_list[13], (D, D), D ** -0.5, 0.21875, ((0, 8),)),
        "back_w": gaussian(key_list[14], (D, CA), D ** -0.5, 0.21875, ((0, 8),)),
    }


epsilon = 1e-05
masked_score = -1e+30

def layer_norm(values):
    centred = values - lax.optimization_barrier(jnp.mean(values, axis=-1, keepdims=True))
    spread = lax.optimization_barrier(jnp.mean(centred * centred, axis=-1, keepdims=True))
    return centred * lax.rsqrt(spread + epsilon)

def rounded(values):
    return lax.optimization_barrier(values.astype(jnp.bfloat16))

def softmax_rows(scores):
    highest = lax.optimization_barrier(jnp.max(scores, axis=-1, keepdims=True))
    raised = jnp.exp(scores - highest)
    return (raised / lax.optimization_barrier(jnp.sum(raised, axis=-1, keepdims=True))).astype(jnp.bfloat16)

def pair_block(tile, trans_in, trans_out, bias_w):
    normed = layer_norm(tile.astype(jnp.float32)).astype(jnp.bfloat16)
    both = jnp.einsum('ijc,cmf->ijmf', normed.astype(jnp.float32), trans_in.astype(jnp.float32))
    hidden = (jax.nn.silu(both[:, :, 0, :]) * both[:, :, 1, :]).astype(jnp.bfloat16)
    update = jnp.einsum('ijf,fc->ijc', hidden.astype(jnp.float32), trans_out.astype(jnp.float32))
    renewed = rounded(tile.astype(jnp.float32) + update)
    renormed = layer_norm(renewed.astype(jnp.float32)).astype(jnp.bfloat16)
    return jnp.einsum('ijc,ch->hij', renormed.astype(jnp.float32), bias_w.astype(jnp.float32)).astype(jnp.bfloat16)

def split_heads(block):
    return block.reshape(TOKENS, HEADS, HEAD).transpose(1, 0, 2)

def one_head(operands):
    query_head, key_head, value_head, bias_head = operands
    scores = jnp.dot(query_head, key_head.T, preferred_element_type=jnp.float32) / math.sqrt(HEAD)
    weights = softmax_rows(scores + bias_head.astype(jnp.float32))
    return jnp.dot(weights, value_head, preferred_element_type=jnp.float32)

def reference(atoms, atom_pair, atom_token, single, pair, atom_w, atom_pair_w, atom_wo, agg_w, trans_in, trans_out, bias_w, token_w, token_wo, back_w):
    rim = (KW - QW) // 2
    atom_norm = layer_norm(atoms.astype(jnp.float32)).astype(jnp.bfloat16)
    projected = jnp.einsum('ac,cmd->amd', atom_norm.astype(jnp.float32), atom_w.astype(jnp.float32)).astype(jnp.bfloat16)
    padded = jnp.pad(projected, ((rim, rim), (0, 0), (0, 0)))
    key_index = (jnp.arange(WINDOWS) * QW)[:, None] + jnp.arange(KW)[None, :]
    window_keys = padded[key_index]
    inside = (key_index >= rim) & (key_index < ATOMS + rim)
    queries = projected[:, 0, :].astype(jnp.float32).reshape(WINDOWS, QW, ATOM_HEADS, ATOM_HEAD)
    key_part = window_keys[:, :, 1, :].astype(jnp.float32).reshape(WINDOWS, KW, ATOM_HEADS, ATOM_HEAD)
    value_part = window_keys[:, :, 2, :].astype(jnp.float32).reshape(WINDOWS, KW, ATOM_HEADS, ATOM_HEAD)
    atom_bias = jnp.einsum('wcij,ch->whij', atom_pair.astype(jnp.float32), atom_pair_w.astype(jnp.float32))
    scores = jnp.einsum('wiha,wjha->whij', queries, key_part) / math.sqrt(ATOM_HEAD) + atom_bias
    scores = jnp.where(inside[:, None, None, :], scores, masked_score)
    weights = softmax_rows(scores)
    attended = jnp.einsum('whij,wjha->wiha', weights.astype(jnp.float32), value_part).reshape(ATOMS, CA)
    gated = (jax.nn.sigmoid(projected[:, 3, :].astype(jnp.float32)) * attended).astype(jnp.bfloat16)
    atoms_mid = rounded(atoms.astype(jnp.float32) + jnp.dot(gated, atom_wo, preferred_element_type=jnp.float32))
    features = jax.nn.relu(jnp.dot(atoms_mid, agg_w, preferred_element_type=jnp.float32)).astype(jnp.bfloat16)
    token_sum = jax.ops.segment_sum(features.astype(jnp.float32), atom_token, num_segments=TOKENS)
    token_count = jax.ops.segment_sum(jnp.ones((ATOMS,), jnp.float32), atom_token, num_segments=TOKENS)
    token_in = rounded(single.astype(jnp.float32) + token_sum / token_count[:, None])
    blocks = pair.reshape(TOKENS // 32, 32, TOKENS, CZ)
    bias_blocks = lax.map(lambda tile: pair_block(tile, trans_in, trans_out, bias_w), blocks)
    pair_bias = jnp.moveaxis(bias_blocks, 1, 0).reshape(HEADS, TOKENS, TOKENS)
    token_norm = layer_norm(token_in.astype(jnp.float32)).astype(jnp.bfloat16)
    token_proj = jnp.einsum('td,dme->tme', token_norm.astype(jnp.float32), token_w.astype(jnp.float32)).astype(jnp.bfloat16)
    heads_out = lax.map(one_head, (split_heads(token_proj[:, 0, :]), split_heads(token_proj[:, 1, :]), split_heads(token_proj[:, 2, :]), pair_bias))
    token_attn = heads_out.transpose(1, 0, 2).reshape(TOKENS, D)
    token_gated = (jax.nn.sigmoid(token_proj[:, 3, :].astype(jnp.float32)) * token_attn).astype(jnp.bfloat16)
    single_out = (token_in.astype(jnp.float32) + jnp.dot(token_gated, token_wo, preferred_element_type=jnp.float32)).astype(jnp.bfloat16)
    atom_back = jnp.dot(single_out, back_w, preferred_element_type=jnp.float32).astype(jnp.bfloat16)
    atoms_out = (atoms_mid.astype(jnp.float32) + atom_back[atom_token].astype(jnp.float32)).astype(jnp.bfloat16)
    return (single_out, atoms_out)
```

```python
import functools
import math

import jax
import jax.numpy as jnp
from jax import lax
from jax.experimental import pallas as pl
from jax.experimental.pallas import tpu as pltpu
from jax.sharding import PartitionSpec as P

HEADS = 16
HEAD = 48
CA = 128
CZ = 128
ATOM_HEADS = 4
ATOM_HEAD = 32
QW = 32
KW = 128


epsilon = 1e-05
masked_score = -1e30


def extended_2(value, sides, width):
    for axis, dim in sides:
        size, length = (lax.axis_size(axis), value.shape[dim])
        up = [(i, (i + 1) % size) for i in range(size - 1)]
        down = [(j, i) for i, j in up]
        last = lax.slice_in_dim(value, length - width, length, axis=dim)
        initial = lax.slice_in_dim(value, 0, width, axis=dim)
        before = lax.ppermute(last, axis, up)
        after = lax.ppermute(initial, axis, down)
        value = jnp.concatenate([before, value, after], axis=dim)
    return value


def layer_norm(values):
    centred = values - jnp.mean(values, axis=-1, keepdims=True)
    spread = jnp.mean(centred * centred, axis=-1, keepdims=True)
    return centred * lax.rsqrt(spread + epsilon)


def rounded(values):
    return lax.optimization_barrier(values.astype(jnp.bfloat16))


def softmax_rows(scores):
    highest = jnp.max(scores, axis=-1, keepdims=True)
    raised = jnp.exp(scores - highest)
    return (raised / jnp.sum(raised, axis=-1, keepdims=True)).astype(jnp.bfloat16)


ROWS_STEP = 16
ROWS_CHAIN = 2


def pair_kernel(
    peers, pair_ref, centre_ref, win_ref, wout_ref, bw_ref, out_ref,
    stage, send, send_sem, recv_sem, own_sem,
):
    step = pl.program_id(0)
    steps = pl.num_programs(0)
    row, col = lax.axis_index("row"), lax.axis_index("col")
    group = send.shape[0] // peers
    width = pair_ref.shape[1]

    def other(k):
        return lax.rem(col + k, peers)

    @pl.when(step == 0)
    def _():
        barrier = pltpu.get_barrier_semaphore()
        for k in range(1, peers):
            pl.semaphore_signal(
                barrier, inc=1, device_id=(row, other(k)), device_id_type=pl.DeviceIdType.MESH
            )
        pl.semaphore_wait(barrier, peers - 1)

    def first(k):
        x = pair_ref[k * ROWS_CHAIN : (k + 1) * ROWS_CHAIN].reshape(ROWS_CHAIN * width, CZ)
        both = lax.dot_general(
            centre_ref[...], x, (((1,), (1,)), ((), ())), preferred_element_type=jnp.float32
        )
        centred = both[:CZ]
        spread = jnp.mean(centred * centred, axis=0, keepdims=True)
        normed = (centred * lax.rsqrt(spread + epsilon)).astype(jnp.bfloat16)
        return centred, both[CZ : CZ + 1], normed

    def second(state):
        centred, average, normed = state
        both = jnp.dot(win_ref[...], normed, preferred_element_type=jnp.float32)
        half = both.shape[0] // 2
        gate = both[:half]
        hidden = ((gate + gate * jnp.tanh(gate)) * both[half:]).astype(jnp.bfloat16)
        return centred + average, hidden

    def third(state):
        tile, hidden = state
        update = jnp.dot(wout_ref[...], hidden, preferred_element_type=jnp.float32)
        renewed = (tile + update).astype(jnp.bfloat16).astype(jnp.float32)
        centred = renewed - jnp.mean(renewed, axis=0, keepdims=True)
        spread = jnp.mean(centred * centred, axis=0, keepdims=True)
        return (centred * lax.rsqrt(spread + epsilon)).astype(jnp.bfloat16)

    def fourth(k, renormed):
        bias = jnp.dot(bw_ref[...], renormed, preferred_element_type=jnp.float32)
        for i in range(ROWS_CHAIN):
            stage[:, k * ROWS_CHAIN + i, :] = bias[:, i * width : (i + 1) * width]

    chains = ROWS_STEP // ROWS_CHAIN
    held = {}
    for turn in range(chains + 3):
        if 0 <= turn - 3:
            fourth(turn - 3, held.pop((2, turn - 3)))
        if 0 <= turn - 2 < chains:
            held[2, turn - 2] = third(held.pop((1, turn - 2)))
        if 0 <= turn - 1 < chains:
            held[1, turn - 1] = second(held.pop((0, turn - 1)))
        if turn < chains:
            held[0, turn] = first(turn)

    rows = pl.ds(pl.multiple_of(step * ROWS_STEP, ROWS_STEP), ROWS_STEP)
    send[:, rows, :] = stage[...].astype(jnp.bfloat16)
    for k in range(1, peers):
        to = other(k)
        pltpu.make_async_remote_copy(
            src_ref=send.at[pl.ds(to * group, group), rows, :],
            dst_ref=out_ref.at[col, :, rows, :],
            send_sem=send_sem.at[k - 1],
            recv_sem=recv_sem.at[k - 1],
            device_id=(row, to),
            device_id_type=pl.DeviceIdType.MESH,
        ).start()

    @pl.when(step == steps - 1)
    def _():
        own = pltpu.make_async_copy(
            send.at[pl.ds(col * group, group)], out_ref.at[col], own_sem
        )
        own.start()
        for k in range(1, peers):
            to = other(k)
            done = pltpu.make_async_remote_copy(
                src_ref=send.at[pl.ds(to * group, group)],
                dst_ref=out_ref.at[lax.rem(col + peers - k, peers)],
                send_sem=send_sem.at[k - 1],
                recv_sem=recv_sem.at[k - 1],
                device_id=(row, to),
                device_id_type=pl.DeviceIdType.MESH,
            )
            done.wait()
        own.wait()


def pair_bias_rows(pair, trans_in, trans_out, bias_w):
    rows, cols, _ = pair.shape
    peers = lax.axis_size("col")
    heads = bias_w.shape[1]
    hidden = trans_in.shape[2]
    eye = jnp.eye(CZ, dtype=jnp.float32) - 1.0 / CZ
    centre = jnp.concatenate([eye, jnp.full((16, CZ), 1.0 / CZ, jnp.float32)]).astype(jnp.bfloat16)
    halved = trans_in * jnp.array([0.5, 1.0], jnp.bfloat16)[None, :, None]
    win = halved.reshape(CZ, 2 * hidden).T
    whole = lambda *shape: pl.BlockSpec(shape, lambda i: (0,) * len(shape))
    return pl.pallas_call(
        functools.partial(pair_kernel, peers),
        grid=(rows // ROWS_STEP,),
        out_shape=jax.ShapeDtypeStruct((peers, heads // peers, rows, cols), jnp.bfloat16),
        in_specs=[
            pl.BlockSpec((ROWS_STEP, cols, CZ), lambda i: (i, 0, 0)),
            whole(CZ + 16, CZ),
            whole(2 * hidden, CZ),
            whole(CZ, hidden),
            whole(heads, CZ),
        ],
        out_specs=pl.BlockSpec(memory_space=pl.ANY),
        scratch_shapes=[
            pltpu.VMEM((heads, ROWS_STEP, cols), jnp.float32),
            pltpu.VMEM((heads, rows, cols), jnp.bfloat16),
            pltpu.SemaphoreType.DMA((peers - 1,)),
            pltpu.SemaphoreType.DMA((peers - 1,)),
            pltpu.SemaphoreType.DMA,
        ],
        compiler_params=pltpu.CompilerParams(
            collective_id=0, has_side_effects=True, vmem_limit_bytes=40 * 2**20,
            dimension_semantics=("arbitrary",),
        ),
        cost_estimate=pl.CostEstimate(
            flops=2 * rows * cols * CZ * (3 * hidden + heads + CZ),
            bytes_accessed=2 * rows * cols * (CZ + 2 * heads),
            transcendentals=rows * cols * hidden,
        ),
        name="pair_bias",
    )(pair, centre, win, trans_out.T, bias_w.T)


def body(
    atoms,
    atom_pair,
    atom_token,
    single,
    pair,
    atom_w,
    atom_pair_w,
    atom_wo,
    agg_w,
    trans_in,
    trans_out,
    bias_w,
    token_w,
    token_wo,
    back_w,
):
    atom_count = atoms.shape[0]
    windows = atom_count // QW
    rim = (KW - QW) // 2
    atom_norm = layer_norm(atoms.astype(jnp.float32)).astype(jnp.bfloat16)
    projected = jnp.einsum(
        "ac,cmd->amd", atom_norm, atom_w, preferred_element_type=jnp.float32
    ).astype(jnp.bfloat16)
    extended = extended_2(atoms, ((("row", "col"), 0),), rim)
    ext_norm = layer_norm(extended.astype(jnp.float32)).astype(jnp.bfloat16)
    key_value = jnp.einsum(
        "ac,cmd->amd", ext_norm, atom_w[:, 1:3, :], preferred_element_type=jnp.float32
    ).astype(jnp.bfloat16)
    device = lax.axis_index(("row", "col"))
    all_atoms = atom_count * lax.axis_size(("row", "col"))
    positions = device * atom_count - rim + jnp.arange(atom_count + 2 * rim)
    inside = (positions >= 0) & (positions < all_atoms)
    window_keys = jnp.stack(
        [
            lax.slice_in_dim(key_value, window * QW, window * QW + KW, axis=0)
            for window in range(windows)
        ]
    )
    window_mask = jnp.stack(
        [
            lax.slice_in_dim(inside, window * QW, window * QW + KW, axis=0)
            for window in range(windows)
        ]
    )
    queries = projected[:, 0, :].reshape(windows, QW, ATOM_HEADS, ATOM_HEAD)
    key_part = window_keys[:, :, 0, :].reshape(windows, KW, ATOM_HEADS, ATOM_HEAD)
    value_part = window_keys[:, :, 1, :].reshape(windows, KW, ATOM_HEADS, ATOM_HEAD)
    atom_bias = jnp.einsum(
        "wcij,ch->whij", atom_pair, atom_pair_w, preferred_element_type=jnp.float32
    )
    scores = (
        jnp.einsum("wiha,wjha->whij", queries, key_part, preferred_element_type=jnp.float32)
        / math.sqrt(ATOM_HEAD)
        + atom_bias
    )
    scores = jnp.where(window_mask[:, None, None, :], scores, masked_score)
    weights = softmax_rows(scores)
    attended = jnp.einsum(
        "whij,wjha->wiha", weights, value_part, preferred_element_type=jnp.float32
    ).reshape(atom_count, CA)
    gated = (jax.nn.sigmoid(projected[:, 3, :].astype(jnp.float32)) * attended).astype(jnp.bfloat16)
    atoms_mid = rounded(
        atoms.astype(jnp.float32) + jnp.dot(gated, atom_wo, preferred_element_type=jnp.float32)
    )
    query_rows = single.shape[0]
    row_start = lax.axis_index("row") * query_rows
    row_atoms = lax.all_gather(atoms_mid, "col", axis=0, tiled=True)
    row_tokens = lax.all_gather(atom_token, "col", axis=0, tiled=True)
    wo_full = lax.all_gather(token_wo, "col", axis=0, tiled=True)
    back_full = lax.all_gather(back_w, "col", axis=0, tiled=True)
    bias_rows = pair_bias_rows(pair, trans_in, trans_out, bias_w)
    slots = jnp.arange(query_rows)
    onehot = (slots[:, None] == (row_tokens - row_start)[None, :]).astype(jnp.bfloat16)
    features = jax.nn.relu(jnp.dot(row_atoms, agg_w, preferred_element_type=jnp.float32)).astype(
        jnp.bfloat16
    )
    token_sum = jnp.dot(onehot, features, preferred_element_type=jnp.float32)
    token_count = jnp.sum(onehot.astype(jnp.float32), axis=1)
    token_in = rounded(single.astype(jnp.float32) + token_sum / token_count[:, None])
    token_norm = layer_norm(token_in.astype(jnp.float32)).astype(jnp.bfloat16)
    head_cols = token_w.shape[2]
    token_proj = (
        jnp.dot(
            token_norm, token_w.reshape(token_w.shape[0], 4 * head_cols),
            preferred_element_type=jnp.float32,
        )
        .astype(jnp.bfloat16)
        .reshape(query_rows, 4, head_cols)
    )
    kv_rows = lax.all_gather(token_proj[:, 1:3, :], "row", axis=0, tiled=True)
    all_tokens = kv_rows.shape[0]
    heads_here = head_cols // HEAD
    query_part = token_proj[:, 0, :].reshape(query_rows, heads_here, HEAD)
    token_keys = kv_rows[:, 0, :].reshape(all_tokens, heads_here, HEAD)
    token_values = kv_rows[:, 1, :].reshape(all_tokens, heads_here, HEAD)
    token_bias = bias_rows.transpose(1, 2, 0, 3).reshape(heads_here, query_rows, all_tokens)
    token_scores = jnp.einsum(
        "ihe,jhe->hij", query_part, token_keys, preferred_element_type=jnp.float32
    ) / math.sqrt(HEAD)
    token_weights = softmax_rows(token_scores + token_bias.astype(jnp.float32))
    token_attn = jnp.einsum(
        "hij,jhe->ihe", token_weights, token_values, preferred_element_type=jnp.float32
    ).reshape(query_rows, head_cols)
    token_gated = (jax.nn.sigmoid(token_proj[:, 3, :].astype(jnp.float32)) * token_attn).astype(
        jnp.bfloat16
    )
    gated_full = lax.all_gather(token_gated, "col", axis=1, tiled=True)
    single_full = (
        token_in.astype(jnp.float32)
        + jnp.dot(gated_full, wo_full, preferred_element_type=jnp.float32)
    ).astype(jnp.bfloat16)
    own_cols = token_wo.shape[0]
    single_out = lax.dynamic_slice_in_dim(
        single_full, lax.axis_index("col") * own_cols, own_cols, 1
    )
    back = jnp.dot(single_full, back_full, preferred_element_type=jnp.float32).astype(jnp.bfloat16)
    own_hot = (slots[None, :] == (atom_token - row_start)[:, None]).astype(jnp.bfloat16)
    picked = jnp.dot(own_hot, back, preferred_element_type=jnp.float32)
    atoms_out = (atoms_mid.astype(jnp.float32) + picked).astype(jnp.bfloat16)
    return (single_out, atoms_out)


def solution(mesh):
    in_specs = (
        P(("row", "col"), None),
        P(("row", "col"), None, None, None),
        P(("row", "col")),
        P("row", None),
        P("row", "col", None),
        P(),
        P(),
        P(),
        P(),
        P(),
        P(),
        P(),
        P(None, None, "col"),
        P("col", None),
        P("col", None),
    )
    out_specs = (P("row", "col"), P(("row", "col"), None))
    return jax.shard_map(body, mesh=mesh, in_specs=in_specs, out_specs=out_specs, check_vma=False)
```

```python
import functools
import math

import jax
import jax.numpy as jnp
from jax import lax
from jax.experimental import pallas as pl
from jax.experimental.pallas import tpu as pltpu
from jax.sharding import PartitionSpec as P

HEADS = 16
HEAD = 48
CA = 128
CZ = 128
ATOM_HEADS = 4
ATOM_HEAD = 32
QW = 32
KW = 128
RIM = (KW - QW) // 2
LANES = 128
ROWS_STEP = 16
ROWS_CHAIN = 2
ATOM_STEP = 1
TOKEN_STEP = 4
MESH = pl.DeviceIdType.MESH


epsilon = 1e-05
masked_score = -1e30


def layer_norm(values):
    centred = values - jnp.mean(values, axis=-1, keepdims=True)
    spread = jnp.mean(centred * centred, axis=-1, keepdims=True)
    return centred * lax.rsqrt(spread + epsilon)


def softmax_rows(scores):
    highest = jnp.max(scores, axis=-1, keepdims=True)
    raised = jnp.exp(scores - highest)
    return (raised / jnp.sum(raised, axis=-1, keepdims=True)).astype(jnp.bfloat16)


def dot(a, b):
    return jnp.dot(a, b, preferred_element_type=jnp.float32)


def dot_rows(a, b):
    return lax.dot_general(a, b, (((1,), (1,)), ((), ())), preferred_element_type=jnp.float32)


def whole_kernel(
    peers, rows_n,
    pair_ref, centre_ref, win_ref, wout_ref, bw_ref,
    atoms_ref, atom_pair_ref, token_ref, single_ref, atom_w_ref, pair_w_ref, atom_wo_ref,
    agg_ref, token_w_ref, wo_ref, back_ref,
    single_out_ref, atoms_out_ref,
    stage, send, bias_all, before, after, mid_all, token_all, hot, token_in, proj, kv_all,
    part_send, part_all, pick_send, pick_all,
    halo_s, halo_r, tok_s, tok_r, mid_s, mid_r, kv_s, kv_r, bias_s, bias_r,
    part_s, part_r, pick_s, pick_r,
):
    step = pl.program_id(0)
    steps = pl.num_programs(0)
    row, col = lax.axis_index("row"), lax.axis_index("col")
    group = send.shape[0] // peers
    width = pair_ref.shape[1]
    atom_count = atoms_ref.shape[0]
    query_rows = single_ref.shape[0]
    own_cols = back_ref.shape[1]

    def other(k):
        return lax.rem(col + k, peers)

    def source(k):
        return lax.rem(col + peers - k, peers)

    def other_row(k):
        return lax.rem(row + k, rows_n)

    def source_row(k):
        return lax.rem(row + rows_n - k, rows_n)

    def to_col(k, src, dst, s, r):
        return pltpu.make_async_remote_copy(
            src_ref=src, dst_ref=dst, send_sem=s.at[k - 1], recv_sem=r.at[k - 1],
            device_id=(row, other(k)), device_id_type=MESH,
        )

    def to_row(k, src, dst):
        return pltpu.make_async_remote_copy(
            src_ref=src, dst_ref=dst, send_sem=kv_s.at[k - 1], recv_sem=kv_r.at[k - 1],
            device_id=(other_row(k), col), device_id_type=MESH,
        )

    is_first = jnp.logical_and(row == 0, col == 0)
    is_last = jnp.logical_and(row == rows_n - 1, col == peers - 1)
    wraps_up = jnp.logical_and(col == peers - 1, row < rows_n - 1)
    wraps_down = jnp.logical_and(col == 0, row > 0)
    up = (lax.rem(jnp.where(col == peers - 1, row + 1, row), rows_n), lax.rem(col + 1, peers))
    down = (
        lax.rem(jnp.where(col == 0, row + rows_n - 1, row), rows_n),
        lax.rem(col + peers - 1, peers),
    )

    def halo_up():
        return pltpu.make_async_remote_copy(
            src_ref=atoms_ref.at[pl.ds(atom_count - RIM, RIM)], dst_ref=before,
            send_sem=halo_s.at[0], recv_sem=halo_r.at[0], device_id=up, device_id_type=MESH,
        )

    def halo_down():
        return pltpu.make_async_remote_copy(
            src_ref=atoms_ref.at[pl.ds(0, RIM)], dst_ref=after,
            send_sem=halo_s.at[1], recv_sem=halo_r.at[1], device_id=down, device_id_type=MESH,
        )

    @pl.when(step == 0)
    def _():
        barrier = pltpu.get_barrier_semaphore()
        for k in range(1, peers):
            pl.semaphore_signal(barrier, inc=1, device_id=(row, other(k)), device_id_type=MESH)
        for k in range(1, rows_n):
            pl.semaphore_signal(barrier, inc=1, device_id=(other_row(k), col), device_id_type=MESH)

        @pl.when(wraps_up)
        def _():
            pl.semaphore_signal(barrier, inc=1, device_id=up, device_id_type=MESH)

        @pl.when(wraps_down)
        def _():
            pl.semaphore_signal(barrier, inc=1, device_id=down, device_id_type=MESH)

        extra = wraps_up.astype(jnp.int32) + wraps_down.astype(jnp.int32)
        pl.semaphore_wait(barrier, peers + rows_n - 2 + extra)

        @pl.when(jnp.logical_not(is_last))
        def _():
            halo_up().start()

        @pl.when(jnp.logical_not(is_first))
        def _():
            halo_down().start()

        @pl.when(is_first)
        def _():
            before[...] = jnp.zeros_like(before)

        @pl.when(is_last)
        def _():
            after[...] = jnp.zeros_like(after)

        token_all[col] = token_ref[...]
        for k in range(1, peers):
            to_col(k, token_ref, token_all.at[col], tok_s, tok_r).start()

    @pl.when(step == ATOM_STEP)
    def _():
        @pl.when(jnp.logical_not(is_last))
        def _():
            halo_up().wait_send()
            halo_down().wait_recv()

        @pl.when(jnp.logical_not(is_first))
        def _():
            halo_down().wait_send()
            halo_up().wait_recv()

        own = atoms_ref[...].astype(jnp.float32)
        extended = jnp.concatenate(
            [before[...].astype(jnp.float32), own, after[...].astype(jnp.float32)]
        )
        projected = dot(layer_norm(extended).astype(jnp.bfloat16), atom_w_ref[...])
        projected = projected.astype(jnp.bfloat16)
        query = projected[RIM : RIM + atom_count, :CA]
        gate = projected[RIM : RIM + atom_count, 3 * CA :].astype(jnp.float32)
        lane = lax.broadcasted_iota(jnp.int32, (QW, CA), 1)
        heads = [
            jnp.logical_and(lane >= h * ATOM_HEAD, lane < (h + 1) * ATOM_HEAD)
            for h in range(ATOM_HEADS)
        ]
        start = (row * peers + col) * atom_count - RIM
        all_atoms = atom_count * peers * rows_n
        spot = lax.broadcasted_iota(jnp.int32, (ATOM_HEADS * QW, KW), 1)
        attended = []
        for window in range(atom_count // QW):
            low = window * QW
            queries = query[low : low + QW].astype(jnp.float32)
            stacked = jnp.concatenate(
                [jnp.where(mask, queries, 0.0) for mask in heads]
            ).astype(jnp.bfloat16)
            planes = [
                atom_pair_ref[window, c].astype(jnp.float32)
                for c in range(atom_pair_ref.shape[1])
            ]
            bias = []
            for h in range(ATOM_HEADS):
                total = planes[0] * pair_w_ref[0, h]
                for c in range(1, len(planes)):
                    total = total + planes[c] * pair_w_ref[c, h]
                bias.append(total)
            scores = dot_rows(stacked, projected[low : low + KW, CA : 2 * CA])
            scores = scores / math.sqrt(ATOM_HEAD) + jnp.concatenate(bias)
            place = spot + (start + low)
            inside = jnp.logical_and(place >= 0, place < all_atoms)
            weights = softmax_rows(jnp.where(inside, scores, masked_score))
            mixed = dot(weights, projected[low : low + KW, 2 * CA : 3 * CA])
            picked = jnp.where(heads[0], mixed[:QW], 0.0)
            for h in range(1, ATOM_HEADS):
                picked = picked + jnp.where(heads[h], mixed[h * QW : (h + 1) * QW], 0.0)
            attended.append(picked)
        gated = (jax.nn.sigmoid(gate) * jnp.concatenate(attended)).astype(jnp.bfloat16)
        mid_all[col] = (own + dot(gated, atom_wo_ref[...])).astype(jnp.bfloat16)
        for k in range(1, peers):
            to_col(k, mid_all.at[col], mid_all.at[col], mid_s, mid_r).start()

    @pl.when(step == TOKEN_STEP)
    def _():
        for k in range(1, peers):
            to_col(k, token_ref, token_all.at[source(k)], tok_s, tok_r).wait()
            to_col(k, mid_all.at[col], mid_all.at[source(k)], mid_s, mid_r).wait()
        slots = lax.broadcasted_iota(jnp.int32, (query_rows, LANES), 0) + row * query_rows
        counts = jnp.zeros((query_rows, LANES), jnp.float32)
        for c in range(peers):
            match = (slots == token_all[c][0:1, :]).astype(jnp.float32)
            counts = counts + match
            hot[:, c * LANES : (c + 1) * LANES] = match.astype(jnp.bfloat16)
        count = jnp.sum(counts, axis=1, keepdims=True)
        mids = mid_all[...].reshape(peers * atom_count, CA)
        features = jnp.maximum(dot(mids, agg_ref[...]), 0.0).astype(jnp.bfloat16)
        sums = dot(hot[...], features)
        held = (single_ref[...].astype(jnp.float32) + sums / count).astype(jnp.bfloat16)
        token_in[...] = held
        normed = layer_norm(held.astype(jnp.float32)).astype(jnp.bfloat16)
        proj[...] = dot(normed, token_w_ref[...]).astype(jnp.bfloat16)
        kv_all[row] = proj[:, LANES : 3 * LANES]
        for k in range(1, rows_n):
            to_row(k, kv_all.at[row], kv_all.at[row]).start()

    def first(k):
        x = pair_ref[k * ROWS_CHAIN : (k + 1) * ROWS_CHAIN].reshape(ROWS_CHAIN * width, CZ)
        both = dot_rows(centre_ref[...], x)
        centred = both[:CZ]
        spread = jnp.mean(centred * centred, axis=0, keepdims=True)
        normed = (centred * lax.rsqrt(spread + epsilon)).astype(jnp.bfloat16)
        return centred, both[CZ : CZ + 1], normed

    def second(state):
        centred, average, normed = state
        both = dot(win_ref[...], normed)
        half = both.shape[0] // 2
        gate = both[:half]
        hidden = ((gate + gate * jnp.tanh(gate)) * both[half:]).astype(jnp.bfloat16)
        return centred + average, hidden

    def third(state):
        tile, hidden = state
        update = dot(wout_ref[...], hidden)
        renewed = (tile + update).astype(jnp.bfloat16).astype(jnp.float32)
        centred = renewed - jnp.mean(renewed, axis=0, keepdims=True)
        spread = jnp.mean(centred * centred, axis=0, keepdims=True)
        return (centred * lax.rsqrt(spread + epsilon)).astype(jnp.bfloat16)

    def fourth(k, renormed):
        bias = dot(bw_ref[...], renormed)
        for i in range(ROWS_CHAIN):
            stage[:, k * ROWS_CHAIN + i, :] = bias[:, i * width : (i + 1) * width]

    chains = ROWS_STEP // ROWS_CHAIN
    held = {}
    for turn in range(chains + 3):
        if 0 <= turn - 3:
            fourth(turn - 3, held.pop((2, turn - 3)))
        if 0 <= turn - 2 < chains:
            held[2, turn - 2] = third(held.pop((1, turn - 2)))
        if 0 <= turn - 1 < chains:
            held[1, turn - 1] = second(held.pop((0, turn - 1)))
        if turn < chains:
            held[0, turn] = first(turn)

    rows = pl.ds(pl.multiple_of(step * ROWS_STEP, ROWS_STEP), ROWS_STEP)
    send[:, rows, :] = stage[...].astype(jnp.bfloat16)
    bias_all[col, :, rows, :] = send[pl.ds(col * group, group), rows, :]
    for k in range(1, peers):
        to_col(
            k, send.at[pl.ds(other(k) * group, group), rows, :], bias_all.at[col, :, rows, :],
            bias_s, bias_r,
        ).start()

    @pl.when(step == steps - 1)
    def _():
        for k in range(1, rows_n):
            to_row(k, kv_all.at[row], kv_all.at[source_row(k)]).wait()
        for k in range(1, peers):
            to_col(
                k, send.at[pl.ds(other(k) * group, group)], bias_all.at[source(k)], bias_s, bias_r
            ).wait()
        query = proj[:, :LANES].astype(jnp.float32)
        keys = kv_all[:, :, :LANES].reshape(rows_n * query_rows, LANES)
        values = kv_all[:, :, LANES:].reshape(rows_n * query_rows, LANES)
        lane = lax.broadcasted_iota(jnp.int32, (query_rows, LANES), 1)
        attended = jnp.zeros((query_rows, LANES), jnp.float32)
        for h in range(group):
            mask = jnp.logical_and(lane >= h * HEAD, lane < (h + 1) * HEAD)
            scores = dot_rows(jnp.where(mask, query, 0.0).astype(jnp.bfloat16), keys)
            bias = jnp.concatenate([bias_all[c, h] for c in range(peers)], axis=1)
            weights = softmax_rows(scores / math.sqrt(HEAD) + bias.astype(jnp.float32))
            attended = attended + jnp.where(mask, dot(weights, values), 0.0)
        gate = proj[:, 3 * LANES :].astype(jnp.float32)
        gated = (jax.nn.sigmoid(gate) * attended).astype(jnp.bfloat16)
        part = dot_rows(wo_ref[...], gated).astype(jnp.bfloat16)
        part_send[...] = part.reshape(peers, own_cols, query_rows)
        for k in range(1, peers):
            to_col(k, part_send.at[other(k)], part_all.at[col], part_s, part_r).start()
        spot = lax.broadcasted_iota(jnp.int32, (own_cols, token_in.shape[1]), 0) + col * own_cols
        column = lax.broadcasted_iota(jnp.int32, (own_cols, token_in.shape[1]), 1)
        chosen = (spot == column).astype(jnp.float32).astype(jnp.bfloat16)
        total = dot_rows(chosen, token_in[...])
        part_all[col] = part_send[col]
        for k in range(1, peers):
            to_col(k, part_send.at[other(k)], part_all.at[source(k)], part_s, part_r).wait()
        update = part_all[0].astype(jnp.float32)
        for c in range(1, peers):
            update = update + part_all[c].astype(jnp.float32)
        fresh = total + update
        single_t = fresh.astype(jnp.bfloat16)
        back = dot(back_ref[...], single_t).astype(jnp.bfloat16)
        picks = dot(back, hot[...]).astype(jnp.bfloat16)
        for c in range(peers):
            pick_send[c] = picks[:, c * LANES : (c + 1) * LANES]
        for k in range(1, peers):
            to_col(k, pick_send.at[other(k)], pick_all.at[col], pick_s, pick_r).start()
        rest = LANES - own_cols
        padded = jnp.concatenate([fresh, jnp.zeros((rest, query_rows), jnp.float32)])
        single_out_ref[...] = padded.T[:, :own_cols].astype(jnp.bfloat16)
        pick_all[col] = pick_send[col]
        for k in range(1, peers):
            to_col(k, pick_send.at[other(k)], pick_all.at[source(k)], pick_s, pick_r).wait()
        total_back = pick_all[0].astype(jnp.float32)
        for c in range(1, peers):
            total_back = total_back + pick_all[c].astype(jnp.float32)
        total_back = total_back.astype(jnp.bfloat16).astype(jnp.float32).T
        atoms_out_ref[...] = (mid_all[col].astype(jnp.float32) + total_back).astype(jnp.bfloat16)


def body(
    atoms, atom_pair, atom_token, single, pair, atom_w, atom_pair_w, atom_wo, agg_w, trans_in,
    trans_out, bias_w, token_w, token_wo, back_w,
):
    rows, cols, _ = pair.shape
    peers, rows_n = lax.axis_size("col"), lax.axis_size("row")
    heads = bias_w.shape[1]
    hidden = trans_in.shape[2]
    atom_count = atoms.shape[0]
    width = single.shape[1]
    own_cols = token_wo.shape[0]
    bf16 = jnp.bfloat16
    eye = jnp.eye(CZ, dtype=jnp.float32) - 1.0 / CZ
    centre = jnp.concatenate([eye, jnp.full((16, CZ), 1.0 / CZ, jnp.float32)]).astype(bf16)
    halved = trans_in * jnp.array([0.5, 1.0], bf16)[None, :, None]
    win = halved.reshape(CZ, 2 * hidden).T
    rest = LANES - own_cols
    token_w_wide = jnp.pad(token_w, ((0, 0), (0, 0), (0, rest))).reshape(width, 4 * LANES)
    wo_t = jnp.pad(token_wo, ((0, rest), (0, 0))).T
    operands = (
        pair, centre, win, trans_out.T, bias_w.T,
        atoms, atom_pair, jnp.broadcast_to(atom_token[None, :], (8, atom_count)), single,
        atom_w.reshape(CA, 4 * CA), atom_pair_w.astype(jnp.float32), atom_wo, agg_w,
        token_w_wide, wo_t, back_w.T,
    )
    whole = lambda value: pl.BlockSpec(value.shape, lambda i, n=value.ndim: (0,) * n)
    in_specs = [pl.BlockSpec((ROWS_STEP, cols, CZ), lambda i: (i, 0, 0))]
    in_specs += [whole(value) for value in operands[1:]]
    in_specs[10] = pl.BlockSpec(memory_space=pltpu.SMEM)
    dma = lambda n: pltpu.SemaphoreType.DMA((n,))
    p, r = peers - 1, rows_n - 1
    return pl.pallas_call(
        functools.partial(whole_kernel, peers, rows_n),
        grid=(rows // ROWS_STEP,),
        out_shape=(
            jax.ShapeDtypeStruct((rows, own_cols), bf16),
            jax.ShapeDtypeStruct((atom_count, CA), bf16),
        ),
        in_specs=in_specs,
        out_specs=(
            pl.BlockSpec((rows, own_cols), lambda i: (0, 0)),
            pl.BlockSpec((atom_count, CA), lambda i: (0, 0)),
        ),
        scratch_shapes=[
            pltpu.VMEM((heads, ROWS_STEP, cols), jnp.float32),
            pltpu.VMEM((heads, rows, cols), bf16),
            pltpu.VMEM((peers, heads // peers, rows, cols), bf16),
            pltpu.VMEM((RIM, CA), bf16),
            pltpu.VMEM((RIM, CA), bf16),
            pltpu.VMEM((peers, atom_count, CA), bf16),
            pltpu.VMEM((peers, 8, atom_count), jnp.int32),
            pltpu.VMEM((rows, peers * atom_count), bf16),
            pltpu.VMEM((rows, width), bf16),
            pltpu.VMEM((rows, 4 * LANES), bf16),
            pltpu.VMEM((rows_n, rows, 2 * LANES), bf16),
            pltpu.VMEM((peers, own_cols, rows), bf16),
            pltpu.VMEM((peers, own_cols, rows), bf16),
            pltpu.VMEM((peers, CA, atom_count), bf16),
            pltpu.VMEM((peers, CA, atom_count), bf16),
            dma(2), dma(2), dma(p), dma(p), dma(p), dma(p), dma(r), dma(r), dma(p), dma(p),
            dma(p), dma(p), dma(p), dma(p),
        ],
        compiler_params=pltpu.CompilerParams(
            collective_id=0, has_side_effects=True, vmem_limit_bytes=56 * 2**20,
            dimension_semantics=("arbitrary",),
        ),
        cost_estimate=pl.CostEstimate(
            flops=2 * rows * cols * CZ * (3 * hidden + heads + CZ),
            bytes_accessed=2 * rows * cols * (CZ + 2 * heads),
            transcendentals=rows * cols * hidden,
        ),
        name="diffusion_block",
    )(*operands)


def solution(mesh):
    in_specs = (
        P(("row", "col"), None),
        P(("row", "col"), None, None, None),
        P(("row", "col")),
        P("row", None),
        P("row", "col", None),
        P(),
        P(),
        P(),
        P(),
        P(),
        P(),
        P(),
        P(None, None, "col"),
        P("col", None),
        P("col", None),
    )
    out_specs = (P("row", "col"), P(("row", "col"), None))
    return jax.shard_map(body, mesh=mesh, in_specs=in_specs, out_specs=out_specs, check_vma=False)
```

```python
import functools
import math

import jax
import jax.numpy as jnp
from jax import lax
from jax.experimental import pallas as pl
from jax.experimental.pallas import tpu as pltpu
from jax.sharding import PartitionSpec as P

HEADS = 16
HEAD = 48
CA = 128
CZ = 128
ATOM_HEADS = 4
ATOM_HEAD = 32
QW = 32
KW = 128
RIM = (KW - QW) // 2
LANES = 128
ROWS_STEP = 16
ROWS_CHAIN = 4
ATOM_STEP = 1
TOKEN_STEP = 4
MESH = pl.DeviceIdType.MESH


epsilon = 1e-05
masked_score = -1e30


def layer_norm(values):
    centred = values - jnp.mean(values, axis=-1, keepdims=True)
    spread = jnp.mean(centred * centred, axis=-1, keepdims=True)
    return centred * lax.rsqrt(spread + epsilon)


def softmax_rows(scores):
    highest = jnp.max(scores, axis=-1, keepdims=True)
    raised = jnp.exp(scores - highest)
    return (raised / jnp.sum(raised, axis=-1, keepdims=True)).astype(jnp.bfloat16)


def dot(a, b):
    return jnp.dot(a, b, preferred_element_type=jnp.float32)


def dot_rows(a, b):
    return lax.dot_general(a, b, (((1,), (1,)), ((), ())), preferred_element_type=jnp.float32)


def whole_kernel(
    peers, rows_n,
    pair_ref, trans_in_ref, trans_out_ref, bw_ref,
    atoms_ref, atom_pair_ref, token_ref, single_ref, atom_w_ref, pair_w_ref, atom_wo_ref,
    agg_ref, token_w_ref, wo_ref, back_ref,
    single_out_ref, atoms_out_ref,
    centre_ref, win_ref, wout_ref, wo_t, back_t, stage, send, bias_all, before, after, mid_all, token_all, hot, token_in, proj, kv_all,
    part_send, part_all, pick_send, pick_all,
    halo_s, halo_r, tok_s, tok_r, mid_s, mid_r, kv_s, kv_r, bias_s, bias_r,
    part_s, part_r, pick_s, pick_r,
):
    step = pl.program_id(0)
    steps = pl.num_programs(0)
    row, col = lax.axis_index("row"), lax.axis_index("col")
    group = send.shape[0] // peers
    width = pair_ref.shape[1]
    atom_count = atoms_ref.shape[0]
    query_rows = single_ref.shape[0]
    own_cols = back_ref.shape[0]

    def other(k):
        return lax.rem(col + k, peers)

    def source(k):
        return lax.rem(col + peers - k, peers)

    def other_row(k):
        return lax.rem(row + k, rows_n)

    def source_row(k):
        return lax.rem(row + rows_n - k, rows_n)

    def to_col(k, src, dst, s, r):
        return pltpu.make_async_remote_copy(
            src_ref=src, dst_ref=dst, send_sem=s.at[k - 1], recv_sem=r.at[k - 1],
            device_id=(row, other(k)), device_id_type=MESH,
        )

    def to_row(k, src, dst):
        return pltpu.make_async_remote_copy(
            src_ref=src, dst_ref=dst, send_sem=kv_s.at[k - 1], recv_sem=kv_r.at[k - 1],
            device_id=(other_row(k), col), device_id_type=MESH,
        )

    is_first = jnp.logical_and(row == 0, col == 0)
    is_last = jnp.logical_and(row == rows_n - 1, col == peers - 1)
    wraps_up = jnp.logical_and(col == peers - 1, row < rows_n - 1)
    wraps_down = jnp.logical_and(col == 0, row > 0)
    up = (lax.rem(jnp.where(col == peers - 1, row + 1, row), rows_n), lax.rem(col + 1, peers))
    down = (
        lax.rem(jnp.where(col == 0, row + rows_n - 1, row), rows_n),
        lax.rem(col + peers - 1, peers),
    )

    def halo_up():
        return pltpu.make_async_remote_copy(
            src_ref=atoms_ref.at[pl.ds(atom_count - RIM, RIM)], dst_ref=before,
            send_sem=halo_s.at[0], recv_sem=halo_r.at[0], device_id=up, device_id_type=MESH,
        )

    def halo_down():
        return pltpu.make_async_remote_copy(
            src_ref=atoms_ref.at[pl.ds(0, RIM)], dst_ref=after,
            send_sem=halo_s.at[1], recv_sem=halo_r.at[1], device_id=down, device_id_type=MESH,
        )

    @pl.when(step == 0)
    def _():
        barrier = pltpu.get_barrier_semaphore()
        for k in range(1, peers):
            pl.semaphore_signal(barrier, inc=1, device_id=(row, other(k)), device_id_type=MESH)
        for k in range(1, rows_n):
            pl.semaphore_signal(barrier, inc=1, device_id=(other_row(k), col), device_id_type=MESH)

        @pl.when(wraps_up)
        def _():
            pl.semaphore_signal(barrier, inc=1, device_id=up, device_id_type=MESH)

        @pl.when(wraps_down)
        def _():
            pl.semaphore_signal(barrier, inc=1, device_id=down, device_id_type=MESH)

        spots = [lax.broadcasted_iota(jnp.int32, (CZ + 16, CZ), d) for d in (0, 1)]
        mean_part = jnp.where(spots[0] < CZ, -1.0 / CZ, 1.0 / CZ)
        centre_ref[...] = (jnp.where(spots[0] == spots[1], 1.0, 0.0) + mean_part).astype(
            jnp.bfloat16
        )
        half = trans_in_ref.shape[2]
        for m, scale in ((0, 0.5), (1, 1.0)):
            block = trans_in_ref[:, m, :].astype(jnp.float32) * scale
            win_ref[m * half : (m + 1) * half, :] = block.T.astype(jnp.bfloat16)
        wout_ref[...] = trans_out_ref[...].astype(jnp.float32).T.astype(jnp.bfloat16)
        back_t[...] = back_ref[...].astype(jnp.float32).T.astype(jnp.bfloat16)
        wide = jnp.concatenate(
            [
                wo_ref[...].astype(jnp.float32),
                jnp.zeros((LANES - own_cols, wo_ref.shape[1]), jnp.float32),
            ]
        )
        wo_t[...] = wide.T.astype(jnp.bfloat16)
        proj[...] = jnp.zeros_like(proj)

        extra = wraps_up.astype(jnp.int32) + wraps_down.astype(jnp.int32)
        pl.semaphore_wait(barrier, peers + rows_n - 2 + extra)

        @pl.when(jnp.logical_not(is_last))
        def _():
            halo_up().start()

        @pl.when(jnp.logical_not(is_first))
        def _():
            halo_down().start()

        @pl.when(is_first)
        def _():
            before[...] = jnp.zeros_like(before)

        @pl.when(is_last)
        def _():
            after[...] = jnp.zeros_like(after)

        token_all[col] = token_ref[...]
        for k in range(1, peers):
            to_col(k, token_ref, token_all.at[col], tok_s, tok_r).start()

    @pl.when(step == ATOM_STEP)
    def _():
        @pl.when(jnp.logical_not(is_last))
        def _():
            halo_up().wait_send()
            halo_down().wait_recv()

        @pl.when(jnp.logical_not(is_first))
        def _():
            halo_down().wait_send()
            halo_up().wait_recv()

        own = atoms_ref[...].astype(jnp.float32)
        extended = jnp.concatenate(
            [before[...].astype(jnp.float32), own, after[...].astype(jnp.float32)]
        )
        normed = layer_norm(extended).astype(jnp.bfloat16)
        query, key, value, gate = [
            dot(normed, atom_w_ref[:, m, :]).astype(jnp.bfloat16) for m in range(4)
        ]
        query = query[RIM : RIM + atom_count]
        gate = gate[RIM : RIM + atom_count].astype(jnp.float32)
        factors = pair_w_ref[...].astype(jnp.float32)
        lane = lax.broadcasted_iota(jnp.int32, (QW, CA), 1)
        heads = [
            jnp.logical_and(lane >= h * ATOM_HEAD, lane < (h + 1) * ATOM_HEAD)
            for h in range(ATOM_HEADS)
        ]
        start = (row * peers + col) * atom_count - RIM
        all_atoms = atom_count * peers * rows_n
        spot = lax.broadcasted_iota(jnp.int32, (ATOM_HEADS * QW, KW), 1)
        attended = []
        for window in range(atom_count // QW):
            low = window * QW
            queries = query[low : low + QW].astype(jnp.float32)
            stacked = jnp.concatenate(
                [jnp.where(mask, queries, 0.0) for mask in heads]
            ).astype(jnp.bfloat16)
            planes = [
                atom_pair_ref[window, c].astype(jnp.float32)
                for c in range(atom_pair_ref.shape[1])
            ]
            bias = []
            for h in range(ATOM_HEADS):
                total = planes[0] * factors[h : h + 1, 0:1]
                for c in range(1, len(planes)):
                    total = total + planes[c] * factors[h : h + 1, c : c + 1]
                bias.append(total)
            scores = dot_rows(stacked, key[low : low + KW])
            scores = scores / math.sqrt(ATOM_HEAD) + jnp.concatenate(bias)
            place = spot + (start + low)
            inside = jnp.logical_and(place >= 0, place < all_atoms)
            weights = softmax_rows(jnp.where(inside, scores, masked_score))
            mixed = dot(weights, value[low : low + KW])
            picked = jnp.where(heads[0], mixed[:QW], 0.0)
            for h in range(1, ATOM_HEADS):
                picked = picked + jnp.where(heads[h], mixed[h * QW : (h + 1) * QW], 0.0)
            attended.append(picked)
        gated = (jax.nn.sigmoid(gate) * jnp.concatenate(attended)).astype(jnp.bfloat16)
        mid_all[col] = (own + dot(gated, atom_wo_ref[...])).astype(jnp.bfloat16)
        for k in range(1, peers):
            to_col(k, mid_all.at[col], mid_all.at[col], mid_s, mid_r).start()

    @pl.when(step == TOKEN_STEP)
    def _():
        for k in range(1, peers):
            to_col(k, token_ref, token_all.at[source(k)], tok_s, tok_r).wait()
            to_col(k, mid_all.at[col], mid_all.at[source(k)], mid_s, mid_r).wait()
        slots = lax.broadcasted_iota(jnp.int32, (query_rows, LANES), 0) + row * query_rows
        counts = jnp.zeros((query_rows, LANES), jnp.float32)
        for c in range(peers):
            match = (slots == token_all[c]).astype(jnp.float32)
            counts = counts + match
            hot[:, c * LANES : (c + 1) * LANES] = match.astype(jnp.bfloat16)
        count = jnp.sum(counts, axis=1, keepdims=True)
        mids = mid_all[...].reshape(peers * atom_count, CA)
        features = jnp.maximum(dot(mids, agg_ref[...]), 0.0).astype(jnp.bfloat16)
        sums = dot(hot[...], features)
        held = (single_ref[...].astype(jnp.float32) + sums / count).astype(jnp.bfloat16)
        token_in[...] = held
        normed = layer_norm(held.astype(jnp.float32)).astype(jnp.bfloat16)
        for m in range(4):
            block = dot_rows(normed, token_w_ref[m]).astype(jnp.bfloat16)
            proj[:, m * LANES : m * LANES + own_cols] = block
        kv_all[row] = proj[:, LANES : 3 * LANES]
        for k in range(1, rows_n):
            to_row(k, kv_all.at[row], kv_all.at[row]).start()

    def first(k):
        x = pair_ref[k * ROWS_CHAIN : (k + 1) * ROWS_CHAIN].reshape(ROWS_CHAIN * width, CZ)
        both = dot_rows(centre_ref[...], x)
        centred = both[:CZ]
        spread = jnp.mean(centred * centred, axis=0, keepdims=True)
        normed = (centred * lax.rsqrt(spread + epsilon)).astype(jnp.bfloat16)
        return centred, both[CZ : CZ + 1], normed

    def second(state):
        centred, average, normed = state
        both = dot(win_ref[...], normed)
        half = both.shape[0] // 2
        gate = both[:half]
        hidden = ((gate + gate * jnp.tanh(gate)) * both[half:]).astype(jnp.bfloat16)
        return centred + average, hidden

    def third(state):
        tile, hidden = state
        update = dot(wout_ref[...], hidden)
        renewed = (tile + update).astype(jnp.bfloat16).astype(jnp.float32)
        centred = renewed - jnp.mean(renewed, axis=0, keepdims=True)
        spread = jnp.mean(centred * centred, axis=0, keepdims=True)
        return (centred * lax.rsqrt(spread + epsilon)).astype(jnp.bfloat16)

    def fourth(k, renormed):
        bias = dot(bw_ref[...], renormed)
        for i in range(ROWS_CHAIN):
            stage[:, k * ROWS_CHAIN + i, :] = bias[:, i * width : (i + 1) * width]

    chains = ROWS_STEP // ROWS_CHAIN
    held = {}
    for turn in range(chains + 3):
        if 0 <= turn - 3:
            fourth(turn - 3, held.pop((2, turn - 3)))
        if 0 <= turn - 2 < chains:
            held[2, turn - 2] = third(held.pop((1, turn - 2)))
        if 0 <= turn - 1 < chains:
            held[1, turn - 1] = second(held.pop((0, turn - 1)))
        if turn < chains:
            held[0, turn] = first(turn)

    rows = pl.ds(pl.multiple_of(step * ROWS_STEP, ROWS_STEP), ROWS_STEP)
    send[:, rows, :] = stage[...].astype(jnp.bfloat16)
    bias_all[col, :, rows, :] = send[pl.ds(col * group, group), rows, :]
    for k in range(1, peers):
        to_col(
            k, send.at[pl.ds(other(k) * group, group), rows, :], bias_all.at[col, :, rows, :],
            bias_s, bias_r,
        ).start()

    @pl.when(step == steps - 1)
    def _():
        for k in range(1, rows_n):
            to_row(k, kv_all.at[row], kv_all.at[source_row(k)]).wait()
        for k in range(1, peers):
            to_col(
                k, send.at[pl.ds(other(k) * group, group)], bias_all.at[source(k)], bias_s, bias_r
            ).wait()
        query = proj[:, :LANES].astype(jnp.float32)
        keys = kv_all[:, :, :LANES].reshape(rows_n * query_rows, LANES)
        values = kv_all[:, :, LANES:].reshape(rows_n * query_rows, LANES)
        lane = lax.broadcasted_iota(jnp.int32, (query_rows, LANES), 1)
        attended = jnp.zeros((query_rows, LANES), jnp.float32)
        for h in range(group):
            mask = jnp.logical_and(lane >= h * HEAD, lane < (h + 1) * HEAD)
            scores = dot_rows(jnp.where(mask, query, 0.0).astype(jnp.bfloat16), keys)
            bias = jnp.concatenate([bias_all[c, h] for c in range(peers)], axis=1)
            weights = softmax_rows(scores / math.sqrt(HEAD) + bias.astype(jnp.float32))
            attended = attended + jnp.where(mask, dot(weights, values), 0.0)
        gate = proj[:, 3 * LANES :].astype(jnp.float32)
        gated = (jax.nn.sigmoid(gate) * attended).astype(jnp.bfloat16)
        part = dot_rows(wo_t[...], gated).astype(jnp.bfloat16)
        part_send[...] = part.reshape(peers, own_cols, query_rows)
        for k in range(1, peers):
            to_col(k, part_send.at[other(k)], part_all.at[col], part_s, part_r).start()
        spot = lax.broadcasted_iota(jnp.int32, (own_cols, token_in.shape[1]), 0) + col * own_cols
        column = lax.broadcasted_iota(jnp.int32, (own_cols, token_in.shape[1]), 1)
        chosen = (spot == column).astype(jnp.float32).astype(jnp.bfloat16)
        total = dot_rows(chosen, token_in[...])
        part_all[col] = part_send[col]
        for k in range(1, peers):
            to_col(k, part_send.at[other(k)], part_all.at[source(k)], part_s, part_r).wait()
        update = part_all[0].astype(jnp.float32)
        for c in range(1, peers):
            update = update + part_all[c].astype(jnp.float32)
        fresh = total + update
        single_t = fresh.astype(jnp.bfloat16)
        back = dot(back_t[...], single_t).astype(jnp.bfloat16)
        picks = dot(back, hot[...]).astype(jnp.bfloat16)
        for c in range(peers):
            pick_send[c] = picks[:, c * LANES : (c + 1) * LANES]
        for k in range(1, peers):
            to_col(k, pick_send.at[other(k)], pick_all.at[col], pick_s, pick_r).start()
        single_out_ref[...] = single_t
        pick_all[col] = pick_send[col]
        for k in range(1, peers):
            to_col(k, pick_send.at[other(k)], pick_all.at[source(k)], pick_s, pick_r).wait()
        total_back = pick_all[0].astype(jnp.float32)
        for c in range(1, peers):
            total_back = total_back + pick_all[c].astype(jnp.float32)
        total_back = total_back.astype(jnp.bfloat16).astype(jnp.float32).T
        atoms_out_ref[...] = (mid_all[col].astype(jnp.float32) + total_back).astype(jnp.bfloat16)


def body(
    atoms, atom_pair, atom_token, single, pair, atom_w, atom_pair_w, atom_wo, agg_w, trans_in,
    trans_out, bias_w, token_w, token_wo, back_w,
):
    rows, cols, _ = pair.shape
    peers, rows_n = lax.axis_size("col"), lax.axis_size("row")
    heads = bias_w.shape[1]
    hidden = trans_in.shape[2]
    atom_count = atoms.shape[0]
    width = single.shape[1]
    own_cols = token_wo.shape[0]
    bf16 = jnp.bfloat16
    operands = (
        pair, trans_in, trans_out, bias_w.T,
        atoms, atom_pair, atom_token[None, :], single, atom_w, atom_pair_w.T, atom_wo, agg_w,
        token_w.transpose(1, 2, 0), token_wo, back_w,
    )
    whole = lambda value: pl.BlockSpec(value.shape, lambda i, n=value.ndim: (0,) * n)
    in_specs = [pl.BlockSpec((ROWS_STEP, cols, CZ), lambda i: (i, 0, 0))]
    in_specs += [whole(value) for value in operands[1:]]
    dma = lambda n: pltpu.SemaphoreType.DMA((n,))
    p, r = peers - 1, rows_n - 1
    single_out, atoms_out = pl.pallas_call(
        functools.partial(whole_kernel, peers, rows_n),
        grid=(rows // ROWS_STEP,),
        out_shape=(
            jax.ShapeDtypeStruct((own_cols, rows), bf16),
            jax.ShapeDtypeStruct((atom_count, CA), bf16),
        ),
        in_specs=in_specs,
        out_specs=(
            pl.BlockSpec((own_cols, rows), lambda i: (0, 0)),
            pl.BlockSpec((atom_count, CA), lambda i: (0, 0)),
        ),
        scratch_shapes=[
            pltpu.VMEM((CZ + 16, CZ), bf16),
            pltpu.VMEM((2 * hidden, CZ), bf16),
            pltpu.VMEM((CZ, hidden), bf16),
            pltpu.VMEM((width, LANES), bf16),
            pltpu.VMEM((CA, own_cols), bf16),
            pltpu.VMEM((heads, ROWS_STEP, cols), jnp.float32),
            pltpu.VMEM((heads, rows, cols), bf16),
            pltpu.VMEM((peers, heads // peers, rows, cols), bf16),
            pltpu.VMEM((RIM, CA), bf16),
            pltpu.VMEM((RIM, CA), bf16),
            pltpu.VMEM((peers, atom_count, CA), bf16),
            pltpu.VMEM((peers, 1, atom_count), jnp.int32),
            pltpu.VMEM((rows, peers * atom_count), bf16),
            pltpu.VMEM((rows, width), bf16),
            pltpu.VMEM((rows, 4 * LANES), bf16),
            pltpu.VMEM((rows_n, rows, 2 * LANES), bf16),
            pltpu.VMEM((peers, own_cols, rows), bf16),
            pltpu.VMEM((peers, own_cols, rows), bf16),
            pltpu.VMEM((peers, CA, atom_count), bf16),
            pltpu.VMEM((peers, CA, atom_count), bf16),
            dma(2), dma(2), dma(p), dma(p), dma(p), dma(p), dma(r), dma(r), dma(p), dma(p),
            dma(p), dma(p), dma(p), dma(p),
        ],
        compiler_params=pltpu.CompilerParams(
            collective_id=0, has_side_effects=True, vmem_limit_bytes=56 * 2**20,
            dimension_semantics=("arbitrary",),
        ),
        cost_estimate=pl.CostEstimate(
            flops=2 * rows * cols * CZ * (3 * hidden + heads + CZ),
            bytes_accessed=2 * rows * cols * (CZ + 2 * heads),
            transcendentals=rows * cols * hidden,
        ),
        name="diffusion_block",
    )(*operands)
    return single_out.T, atoms_out


def solution(mesh):
    in_specs = (
        P(("row", "col"), None),
        P(("row", "col"), None, None, None),
        P(("row", "col")),
        P("row", None),
        P("row", "col", None),
        P(),
        P(),
        P(),
        P(),
        P(),
        P(),
        P(),
        P(None, None, "col"),
        P("col", None),
        P("col", None),
    )
    out_specs = (P("row", "col"), P(("row", "col"), None))
    return jax.shard_map(body, mesh=mesh, in_specs=in_specs, out_specs=out_specs, check_vma=False)
```

```python
import functools
import math

import jax
import jax.numpy as jnp
from jax import lax
from jax.experimental import pallas as pl
from jax.experimental.pallas import tpu as pltpu
from jax.sharding import PartitionSpec as P

HEADS = 16
HEAD = 48
CA = 128
CZ = 128
ATOM_HEADS = 4
ATOM_HEAD = 32
QW = 32
KW = 128
RIM = (KW - QW) // 2
LANES = 128
ROWS_STEP = 32
ROWS_CHAIN = 4
ATOM_STEP = 1
TOKEN_STEP = 3
MESH = pl.DeviceIdType.MESH


epsilon = 1e-05
masked_score = -1e30


def layer_norm(values):
    centred = values - jnp.mean(values, axis=-1, keepdims=True)
    spread = jnp.mean(centred * centred, axis=-1, keepdims=True)
    return centred * lax.rsqrt(spread + epsilon)


def softmax_rows(scores):
    highest = jnp.max(scores, axis=-1, keepdims=True)
    raised = jnp.exp(scores - highest)
    return (raised * (1.0 / jnp.sum(raised, axis=-1, keepdims=True))).astype(jnp.bfloat16)


def dot(a, b):
    return jnp.dot(a, b, preferred_element_type=jnp.float32)


def dot_rows(a, b):
    return lax.dot_general(a, b, (((1,), (1,)), ((), ())), preferred_element_type=jnp.float32)


def whole_kernel(
    peers, rows_n,
    pair_ref, trans_in_ref, trans_out_ref, bw_ref,
    atoms_ref, atom_pair_ref, token_ref, single_ref, atom_w_ref, pair_w_ref, atom_wo_ref,
    agg_ref, token_w_ref, wo_ref, back_ref,
    single_out_ref, atoms_out_ref,
    centre_ref, win_ref, wout_ref, wo_t, back_t, stage, send, bias_all, before, after, mid_all, token_all, hot, token_in, proj, kv_all,
    part_send, part_all, pick_send, pick_all,
    halo_s, halo_r, tok_s, tok_r, mid_s, mid_r, kv_s, kv_r, bias_s, bias_r,
    part_s, part_r, pick_s, pick_r,
):
    step = pl.program_id(0)
    steps = pl.num_programs(0)
    row, col = lax.axis_index("row"), lax.axis_index("col")
    group = send.shape[0] // peers
    width = pair_ref.shape[1]
    atom_count = atoms_ref.shape[0]
    query_rows = single_ref.shape[0]
    own_cols = back_ref.shape[0]

    def other(k):
        return lax.rem(col + k, peers)

    def source(k):
        return lax.rem(col + peers - k, peers)

    def other_row(k):
        return lax.rem(row + k, rows_n)

    def source_row(k):
        return lax.rem(row + rows_n - k, rows_n)

    def to_col(k, src, dst, s, r):
        return pltpu.make_async_remote_copy(
            src_ref=src, dst_ref=dst, send_sem=s.at[k - 1], recv_sem=r.at[k - 1],
            device_id=(row, other(k)), device_id_type=MESH,
        )

    def to_row(k, src, dst):
        return pltpu.make_async_remote_copy(
            src_ref=src, dst_ref=dst, send_sem=kv_s.at[k - 1], recv_sem=kv_r.at[k - 1],
            device_id=(other_row(k), col), device_id_type=MESH,
        )

    is_first = jnp.logical_and(row == 0, col == 0)
    is_last = jnp.logical_and(row == rows_n - 1, col == peers - 1)
    wraps_up = jnp.logical_and(col == peers - 1, row < rows_n - 1)
    wraps_down = jnp.logical_and(col == 0, row > 0)
    up = (lax.rem(jnp.where(col == peers - 1, row + 1, row), rows_n), lax.rem(col + 1, peers))
    down = (
        lax.rem(jnp.where(col == 0, row + rows_n - 1, row), rows_n),
        lax.rem(col + peers - 1, peers),
    )

    def halo_up():
        return pltpu.make_async_remote_copy(
            src_ref=atoms_ref.at[pl.ds(atom_count - RIM, RIM)], dst_ref=before,
            send_sem=halo_s.at[0], recv_sem=halo_r.at[0], device_id=up, device_id_type=MESH,
        )

    def halo_down():
        return pltpu.make_async_remote_copy(
            src_ref=atoms_ref.at[pl.ds(0, RIM)], dst_ref=after,
            send_sem=halo_s.at[1], recv_sem=halo_r.at[1], device_id=down, device_id_type=MESH,
        )

    @pl.when(step == 0)
    def _():
        barrier = pltpu.get_barrier_semaphore()
        for k in range(1, peers):
            pl.semaphore_signal(barrier, inc=1, device_id=(row, other(k)), device_id_type=MESH)
        for k in range(1, rows_n):
            pl.semaphore_signal(barrier, inc=1, device_id=(other_row(k), col), device_id_type=MESH)

        @pl.when(wraps_up)
        def _():
            pl.semaphore_signal(barrier, inc=1, device_id=up, device_id_type=MESH)

        @pl.when(wraps_down)
        def _():
            pl.semaphore_signal(barrier, inc=1, device_id=down, device_id_type=MESH)

        spots = [lax.broadcasted_iota(jnp.int32, (CZ + 16, CZ), d) for d in (0, 1)]
        mean_part = jnp.where(spots[0] < CZ, -1.0 / CZ, 1.0 / CZ)
        centre_ref[...] = (jnp.where(spots[0] == spots[1], 1.0, 0.0) + mean_part).astype(
            jnp.bfloat16
        )
        half = trans_in_ref.shape[2]
        for m, scale in ((0, 0.5), (1, 1.0)):
            block = trans_in_ref[:, m, :].astype(jnp.float32) * scale
            win_ref[m * half : (m + 1) * half, :] = block.T.astype(jnp.bfloat16)
        wout_ref[...] = trans_out_ref[...].astype(jnp.float32).T.astype(jnp.bfloat16)
        back_t[...] = back_ref[...].astype(jnp.float32).T.astype(jnp.bfloat16)
        wide = jnp.concatenate(
            [
                wo_ref[...].astype(jnp.float32),
                jnp.zeros((LANES - own_cols, wo_ref.shape[1]), jnp.float32),
            ]
        )
        wo_t[...] = wide.T.astype(jnp.bfloat16)
        proj[...] = jnp.zeros_like(proj)

        extra = wraps_up.astype(jnp.int32) + wraps_down.astype(jnp.int32)
        pl.semaphore_wait(barrier, peers + rows_n - 2 + extra)

        @pl.when(jnp.logical_not(is_last))
        def _():
            halo_up().start()

        @pl.when(jnp.logical_not(is_first))
        def _():
            halo_down().start()

        @pl.when(is_first)
        def _():
            before[...] = jnp.zeros_like(before)

        @pl.when(is_last)
        def _():
            after[...] = jnp.zeros_like(after)

        token_all[col] = token_ref[...]
        for k in range(1, peers):
            to_col(k, token_ref, token_all.at[col], tok_s, tok_r).start()

    @pl.when(step == ATOM_STEP)
    def _():
        @pl.when(jnp.logical_not(is_last))
        def _():
            halo_up().wait_send()
            halo_down().wait_recv()

        @pl.when(jnp.logical_not(is_first))
        def _():
            halo_down().wait_send()
            halo_up().wait_recv()

        own = atoms_ref[...].astype(jnp.float32)
        extended = jnp.concatenate(
            [before[...].astype(jnp.float32), own, after[...].astype(jnp.float32)]
        )
        normed = layer_norm(extended).astype(jnp.bfloat16)
        query, key, value, gate = [
            dot(normed, atom_w_ref[:, m, :]).astype(jnp.bfloat16) for m in range(4)
        ]
        query = query[RIM : RIM + atom_count]
        gate = gate[RIM : RIM + atom_count].astype(jnp.float32)
        factors = pair_w_ref[...].astype(jnp.float32)
        lane = lax.broadcasted_iota(jnp.int32, (QW, CA), 1)
        heads = [
            jnp.logical_and(lane >= h * ATOM_HEAD, lane < (h + 1) * ATOM_HEAD)
            for h in range(ATOM_HEADS)
        ]
        start = (row * peers + col) * atom_count - RIM
        all_atoms = atom_count * peers * rows_n
        spot = lax.broadcasted_iota(jnp.int32, (ATOM_HEADS * QW, KW), 1)
        attended = []
        for window in range(atom_count // QW):
            low = window * QW
            queries = query[low : low + QW].astype(jnp.float32)
            stacked = jnp.concatenate(
                [jnp.where(mask, queries, 0.0) for mask in heads]
            ).astype(jnp.bfloat16)
            planes = [
                atom_pair_ref[window, c].astype(jnp.float32)
                for c in range(atom_pair_ref.shape[1])
            ]
            bias = []
            for h in range(ATOM_HEADS):
                total = planes[0] * factors[h : h + 1, 0:1]
                for c in range(1, len(planes)):
                    total = total + planes[c] * factors[h : h + 1, c : c + 1]
                bias.append(total)
            scores = dot_rows(stacked, key[low : low + KW])
            scores = scores * (1.0 / math.sqrt(ATOM_HEAD)) + jnp.concatenate(bias)
            place = spot + (start + low)
            inside = jnp.logical_and(place >= 0, place < all_atoms)
            weights = softmax_rows(jnp.where(inside, scores, masked_score))
            mixed = dot(weights, value[low : low + KW])
            picked = jnp.where(heads[0], mixed[:QW], 0.0)
            for h in range(1, ATOM_HEADS):
                picked = picked + jnp.where(heads[h], mixed[h * QW : (h + 1) * QW], 0.0)
            attended.append(picked)
        gated = (jax.nn.sigmoid(gate) * jnp.concatenate(attended)).astype(jnp.bfloat16)
        mid_all[col] = (own + dot(gated, atom_wo_ref[...])).astype(jnp.bfloat16)
        for k in range(1, peers):
            to_col(k, mid_all.at[col], mid_all.at[col], mid_s, mid_r).start()

    @pl.when(step == TOKEN_STEP)
    def _():
        for k in range(1, peers):
            to_col(k, token_ref, token_all.at[source(k)], tok_s, tok_r).wait()
            to_col(k, mid_all.at[col], mid_all.at[source(k)], mid_s, mid_r).wait()
        slots = lax.broadcasted_iota(jnp.int32, (query_rows, LANES), 0) + row * query_rows
        counts = jnp.zeros((query_rows, LANES), jnp.float32)
        for c in range(peers):
            match = (slots == token_all[c]).astype(jnp.float32)
            counts = counts + match
            hot[:, c * LANES : (c + 1) * LANES] = match.astype(jnp.bfloat16)
        count = jnp.sum(counts, axis=1, keepdims=True)
        mids = mid_all[...].reshape(peers * atom_count, CA)
        features = jnp.maximum(dot(mids, agg_ref[...]), 0.0).astype(jnp.bfloat16)
        sums = dot(hot[...], features)
        held = (single_ref[...].astype(jnp.float32) + sums * (1.0 / count)).astype(jnp.bfloat16)
        token_in[...] = held
        normed = layer_norm(held.astype(jnp.float32)).astype(jnp.bfloat16)
        for m in range(4):
            block = dot_rows(normed, token_w_ref[m]).astype(jnp.bfloat16)
            proj[:, m * LANES : m * LANES + own_cols] = block
        kv_all[row] = proj[:, LANES : 3 * LANES]
        for k in range(1, rows_n):
            to_row(k, kv_all.at[row], kv_all.at[row]).start()

    def first(k):
        x = pair_ref[k * ROWS_CHAIN : (k + 1) * ROWS_CHAIN].reshape(ROWS_CHAIN * width, CZ)
        both = dot_rows(centre_ref[...], x)
        centred = both[:CZ]
        spread = jnp.mean(centred * centred, axis=0, keepdims=True)
        normed = (centred * lax.rsqrt(spread + epsilon)).astype(jnp.bfloat16)
        return centred, both[CZ : CZ + 1], normed

    def second(state):
        centred, average, normed = state
        both = dot(win_ref[...], normed)
        half = both.shape[0] // 2
        gate = both[:half]
        hidden = ((gate + gate * jnp.tanh(gate)) * both[half:]).astype(jnp.bfloat16)
        return centred + average, hidden

    def third(state):
        tile, hidden = state
        update = dot(wout_ref[...], hidden)
        renewed = (tile + update).astype(jnp.bfloat16).astype(jnp.float32)
        centred = renewed - jnp.mean(renewed, axis=0, keepdims=True)
        spread = jnp.mean(centred * centred, axis=0, keepdims=True)
        return (centred * lax.rsqrt(spread + epsilon)).astype(jnp.bfloat16)

    def fourth(k, renormed):
        bias = dot(bw_ref[...], renormed)
        for i in range(ROWS_CHAIN):
            stage[:, k * ROWS_CHAIN + i, :] = bias[:, i * width : (i + 1) * width]

    chains = ROWS_STEP // ROWS_CHAIN
    held = {}
    for turn in range(chains + 3):
        if 0 <= turn - 3:
            fourth(turn - 3, held.pop((2, turn - 3)))
        if 0 <= turn - 2 < chains:
            held[2, turn - 2] = third(held.pop((1, turn - 2)))
        if 0 <= turn - 1 < chains:
            held[1, turn - 1] = second(held.pop((0, turn - 1)))
        if turn < chains:
            held[0, turn] = first(turn)

    rows = pl.ds(pl.multiple_of(step * ROWS_STEP, ROWS_STEP), ROWS_STEP)
    send[:, rows, :] = stage[...].astype(jnp.bfloat16)
    bias_all[col, :, rows, :] = send[pl.ds(col * group, group), rows, :]
    for k in range(1, peers):
        to_col(
            k, send.at[pl.ds(other(k) * group, group), rows, :], bias_all.at[col, :, rows, :],
            bias_s, bias_r,
        ).start()

    @pl.when(step == steps - 1)
    def _():
        for k in range(1, rows_n):
            to_row(k, kv_all.at[row], kv_all.at[source_row(k)]).wait()
        for k in range(1, peers):
            to_col(
                k, send.at[pl.ds(other(k) * group, group)], bias_all.at[source(k)], bias_s, bias_r
            ).wait()
        query = proj[:, :LANES].astype(jnp.float32)
        keys = kv_all[:, :, :LANES].reshape(rows_n * query_rows, LANES)
        values = kv_all[:, :, LANES:].reshape(rows_n * query_rows, LANES)
        lane = lax.broadcasted_iota(jnp.int32, (query_rows, LANES), 1)
        attended = jnp.zeros((query_rows, LANES), jnp.float32)
        for h in range(group):
            mask = jnp.logical_and(lane >= h * HEAD, lane < (h + 1) * HEAD)
            scores = dot_rows(jnp.where(mask, query, 0.0).astype(jnp.bfloat16), keys)
            bias = jnp.concatenate([bias_all[c, h] for c in range(peers)], axis=1)
            weights = softmax_rows(scores * (1.0 / math.sqrt(HEAD)) + bias.astype(jnp.float32))
            attended = attended + jnp.where(mask, dot(weights, values), 0.0)
        gate = proj[:, 3 * LANES :].astype(jnp.float32)
        gated = (jax.nn.sigmoid(gate) * attended).astype(jnp.bfloat16)
        part = dot_rows(wo_t[...], gated).astype(jnp.bfloat16)
        part_send[...] = part.reshape(peers, own_cols, query_rows)
        for k in range(1, peers):
            to_col(k, part_send.at[other(k)], part_all.at[col], part_s, part_r).start()
        spot = lax.broadcasted_iota(jnp.int32, (own_cols, token_in.shape[1]), 0) + col * own_cols
        column = lax.broadcasted_iota(jnp.int32, (own_cols, token_in.shape[1]), 1)
        chosen = (spot == column).astype(jnp.float32).astype(jnp.bfloat16)
        total = dot_rows(chosen, token_in[...])
        part_all[col] = part_send[col]
        for k in range(1, peers):
            to_col(k, part_send.at[other(k)], part_all.at[source(k)], part_s, part_r).wait()
        update = part_all[0].astype(jnp.float32)
        for c in range(1, peers):
            update = update + part_all[c].astype(jnp.float32)
        fresh = total + update
        single_t = fresh.astype(jnp.bfloat16)
        back = dot(back_t[...], single_t).astype(jnp.bfloat16)
        picks = dot(back, hot[...]).astype(jnp.bfloat16)
        for c in range(peers):
            pick_send[c] = picks[:, c * LANES : (c + 1) * LANES]
        for k in range(1, peers):
            to_col(k, pick_send.at[other(k)], pick_all.at[col], pick_s, pick_r).start()
        single_out_ref[...] = single_t
        pick_all[col] = pick_send[col]
        for k in range(1, peers):
            to_col(k, pick_send.at[other(k)], pick_all.at[source(k)], pick_s, pick_r).wait()
        total_back = pick_all[0].astype(jnp.float32)
        for c in range(1, peers):
            total_back = total_back + pick_all[c].astype(jnp.float32)
        total_back = total_back.astype(jnp.bfloat16).astype(jnp.float32).T
        atoms_out_ref[...] = (mid_all[col].astype(jnp.float32) + total_back).astype(jnp.bfloat16)


def body(
    atoms, atom_pair, atom_token, single, pair, atom_w, atom_pair_w, atom_wo, agg_w, trans_in,
    trans_out, bias_w, token_w, token_wo, back_w,
):
    rows, cols, _ = pair.shape
    peers, rows_n = lax.axis_size("col"), lax.axis_size("row")
    heads = bias_w.shape[1]
    hidden = trans_in.shape[2]
    atom_count = atoms.shape[0]
    width = single.shape[1]
    own_cols = token_wo.shape[0]
    bf16 = jnp.bfloat16
    operands = (
        pair, trans_in, trans_out, bias_w.T,
        atoms, atom_pair, atom_token[None, :], single, atom_w, atom_pair_w.T, atom_wo, agg_w,
        token_w.transpose(1, 2, 0), token_wo, back_w,
    )
    whole = lambda value: pl.BlockSpec(value.shape, lambda i, n=value.ndim: (0,) * n)
    in_specs = [pl.BlockSpec((ROWS_STEP, cols, CZ), lambda i: (i, 0, 0))]
    in_specs += [whole(value) for value in operands[1:]]
    dma = lambda n: pltpu.SemaphoreType.DMA((n,))
    p, r = peers - 1, rows_n - 1
    single_out, atoms_out = pl.pallas_call(
        functools.partial(whole_kernel, peers, rows_n),
        grid=(rows // ROWS_STEP,),
        out_shape=(
            jax.ShapeDtypeStruct((own_cols, rows), bf16),
            jax.ShapeDtypeStruct((atom_count, CA), bf16),
        ),
        in_specs=in_specs,
        out_specs=(
            pl.BlockSpec((own_cols, rows), lambda i: (0, 0)),
            pl.BlockSpec((atom_count, CA), lambda i: (0, 0)),
        ),
        scratch_shapes=[
            pltpu.VMEM((CZ + 16, CZ), bf16),
            pltpu.VMEM((2 * hidden, CZ), bf16),
            pltpu.VMEM((CZ, hidden), bf16),
            pltpu.VMEM((width, LANES), bf16),
            pltpu.VMEM((CA, own_cols), bf16),
            pltpu.VMEM((heads, ROWS_STEP, cols), jnp.float32),
            pltpu.VMEM((heads, rows, cols), bf16),
            pltpu.VMEM((peers, heads // peers, rows, cols), bf16),
            pltpu.VMEM((RIM, CA), bf16),
            pltpu.VMEM((RIM, CA), bf16),
            pltpu.VMEM((peers, atom_count, CA), bf16),
            pltpu.VMEM((peers, 1, atom_count), jnp.int32),
            pltpu.VMEM((rows, peers * atom_count), bf16),
            pltpu.VMEM((rows, width), bf16),
            pltpu.VMEM((rows, 4 * LANES), bf16),
            pltpu.VMEM((rows_n, rows, 2 * LANES), bf16),
            pltpu.VMEM((peers, own_cols, rows), bf16),
            pltpu.VMEM((peers, own_cols, rows), bf16),
            pltpu.VMEM((peers, CA, atom_count), bf16),
            pltpu.VMEM((peers, CA, atom_count), bf16),
            dma(2), dma(2), dma(p), dma(p), dma(p), dma(p), dma(r), dma(r), dma(p), dma(p),
            dma(p), dma(p), dma(p), dma(p),
        ],
        compiler_params=pltpu.CompilerParams(
            collective_id=0, has_side_effects=True, vmem_limit_bytes=56 * 2**20,
            dimension_semantics=("arbitrary",),
        ),
        cost_estimate=pl.CostEstimate(
            flops=2 * rows * cols * CZ * (3 * hidden + heads + CZ),
            bytes_accessed=2 * rows * cols * (CZ + 2 * heads),
            transcendentals=rows * cols * hidden,
        ),
        name="diffusion_block",
    )(*operands)
    return single_out.T, atoms_out


def solution(mesh):
    in_specs = (
        P(("row", "col"), None),
        P(("row", "col"), None, None, None),
        P(("row", "col")),
        P("row", None),
        P("row", "col", None),
        P(),
        P(),
        P(),
        P(),
        P(),
        P(),
        P(),
        P(None, None, "col"),
        P("col", None),
        P("col", None),
    )
    out_specs = (P("row", "col"), P(("row", "col"), None))
    return jax.shard_map(body, mesh=mesh, in_specs=in_specs, out_specs=out_specs, check_vma=False)
```

```python
import functools
import math

import jax
import jax.numpy as jnp
from jax import lax
from jax.experimental import pallas as pl
from jax.experimental.pallas import tpu as pltpu
from jax.sharding import PartitionSpec as P

HEADS = 16
HEAD = 48
CA = 128
CZ = 128
ATOM_HEADS = 4
ATOM_HEAD = 32
QW = 32
KW = 128
RIM = (KW - QW) // 2
LANES = 128
ROWS_STEP = 32
ROWS_CHAIN = 4
ATOM_STEP = 1
TOKEN_STEP = 3
BLOCK_ROWS = 64
ATTEND_STEPS = (4, 5, 7)
FINISH_STEPS = (6, 7)
MESH = pl.DeviceIdType.MESH


epsilon = 1e-05
masked_score = -1e30


def layer_norm(values):
    centred = values - jnp.mean(values, axis=-1, keepdims=True)
    spread = jnp.mean(centred * centred, axis=-1, keepdims=True)
    return centred * lax.rsqrt(spread + epsilon)


def softmax_rows(scores):
    highest = jnp.max(scores, axis=-1, keepdims=True)
    raised = jnp.exp(scores - highest)
    return (raised * (1.0 / jnp.sum(raised, axis=-1, keepdims=True))).astype(jnp.bfloat16)


def dot(a, b):
    return jnp.dot(a, b, preferred_element_type=jnp.float32)


def dot_rows(a, b):
    return lax.dot_general(a, b, (((1,), (1,)), ((), ())), preferred_element_type=jnp.float32)


def whole_kernel(
    peers, rows_n,
    pair_ref, trans_in_ref, trans_out_ref, bw_ref,
    atoms_ref, atom_pair_ref, token_ref, single_ref, atom_w_ref, pair_w_ref, atom_wo_ref,
    agg_ref, token_w_ref, wo_ref, back_ref,
    single_out_ref, atoms_out_ref,
    centre_ref, win_ref, wout_ref, wo_wide, back_t, own_in, single_rows, stage, send, bias_all, before, after, mid_all, token_all, hot, proj, kv_all,
    part_send, part_all, pick_send, pick_all,
    halo_s, halo_r, tok_s, tok_r, mid_s, mid_r, kv_s, kv_r, bias_s, bias_r,
    part_s, part_r, pick_s, pick_r,
):
    step = pl.program_id(0)
    steps = pl.num_programs(0)
    row, col = lax.axis_index("row"), lax.axis_index("col")
    group = send.shape[0] // peers
    width = pair_ref.shape[1]
    atom_count = atoms_ref.shape[0]
    query_rows = single_ref.shape[0]
    own_cols = back_ref.shape[0]

    def other(k):
        return lax.rem(col + k, peers)

    def source(k):
        return lax.rem(col + peers - k, peers)

    def other_row(k):
        return lax.rem(row + k, rows_n)

    def source_row(k):
        return lax.rem(row + rows_n - k, rows_n)

    def to_col(k, src, dst, s, r, base=0):
        return pltpu.make_async_remote_copy(
            src_ref=src, dst_ref=dst, send_sem=s.at[base + k - 1],
            recv_sem=r.at[base + k - 1], device_id=(row, other(k)), device_id_type=MESH,
        )

    def to_row(k, src, dst):
        return pltpu.make_async_remote_copy(
            src_ref=src, dst_ref=dst, send_sem=kv_s.at[k - 1], recv_sem=kv_r.at[k - 1],
            device_id=(other_row(k), col), device_id_type=MESH,
        )

    is_first = jnp.logical_and(row == 0, col == 0)
    is_last = jnp.logical_and(row == rows_n - 1, col == peers - 1)
    wraps_up = jnp.logical_and(col == peers - 1, row < rows_n - 1)
    wraps_down = jnp.logical_and(col == 0, row > 0)
    up = (lax.rem(jnp.where(col == peers - 1, row + 1, row), rows_n), lax.rem(col + 1, peers))
    down = (
        lax.rem(jnp.where(col == 0, row + rows_n - 1, row), rows_n),
        lax.rem(col + peers - 1, peers),
    )

    def halo_up():
        return pltpu.make_async_remote_copy(
            src_ref=atoms_ref.at[pl.ds(atom_count - RIM, RIM)], dst_ref=before,
            send_sem=halo_s.at[0], recv_sem=halo_r.at[0], device_id=up, device_id_type=MESH,
        )

    def halo_down():
        return pltpu.make_async_remote_copy(
            src_ref=atoms_ref.at[pl.ds(0, RIM)], dst_ref=after,
            send_sem=halo_s.at[1], recv_sem=halo_r.at[1], device_id=down, device_id_type=MESH,
        )

    @pl.when(step == 0)
    def _():
        barrier = pltpu.get_barrier_semaphore()
        for k in range(1, peers):
            pl.semaphore_signal(barrier, inc=1, device_id=(row, other(k)), device_id_type=MESH)
        for k in range(1, rows_n):
            pl.semaphore_signal(barrier, inc=1, device_id=(other_row(k), col), device_id_type=MESH)

        @pl.when(wraps_up)
        def _():
            pl.semaphore_signal(barrier, inc=1, device_id=up, device_id_type=MESH)

        @pl.when(wraps_down)
        def _():
            pl.semaphore_signal(barrier, inc=1, device_id=down, device_id_type=MESH)

        spots = [lax.broadcasted_iota(jnp.int32, (CZ + 16, CZ), d) for d in (0, 1)]
        mean_part = jnp.where(spots[0] < CZ, -1.0 / CZ, 1.0 / CZ)
        centre_ref[...] = (jnp.where(spots[0] == spots[1], 1.0, 0.0) + mean_part).astype(
            jnp.bfloat16
        )
        half = trans_in_ref.shape[2]
        for m, scale in ((0, 0.5), (1, 1.0)):
            block = trans_in_ref[:, m, :].astype(jnp.float32) * scale
            win_ref[m * half : (m + 1) * half, :] = block.T.astype(jnp.bfloat16)
        wout_ref[...] = trans_out_ref[...].astype(jnp.float32).T.astype(jnp.bfloat16)
        back_t[...] = jnp.zeros_like(back_t)
        back_t[:, :own_cols] = back_ref[...].astype(jnp.float32).T.astype(jnp.bfloat16)
        wo_wide[...] = jnp.zeros_like(wo_wide)
        plain = wo_ref[...].astype(jnp.float32)
        for c in range(peers):
            block = plain[:, c * own_cols : (c + 1) * own_cols]
            wo_wide[:own_cols, c * LANES : c * LANES + own_cols] = block.astype(jnp.bfloat16)
        proj[...] = jnp.zeros_like(proj)

        extra = wraps_up.astype(jnp.int32) + wraps_down.astype(jnp.int32)
        pl.semaphore_wait(barrier, peers + rows_n - 2 + extra)

        @pl.when(jnp.logical_not(is_last))
        def _():
            halo_up().start()

        @pl.when(jnp.logical_not(is_first))
        def _():
            halo_down().start()

        @pl.when(is_first)
        def _():
            before[...] = jnp.zeros_like(before)

        @pl.when(is_last)
        def _():
            after[...] = jnp.zeros_like(after)

        token_all[col] = token_ref[...]
        for k in range(1, peers):
            to_col(k, token_ref, token_all.at[col], tok_s, tok_r).start()

    @pl.when(step == ATOM_STEP)
    def _():
        @pl.when(jnp.logical_not(is_last))
        def _():
            halo_up().wait_send()
            halo_down().wait_recv()

        @pl.when(jnp.logical_not(is_first))
        def _():
            halo_down().wait_send()
            halo_up().wait_recv()

        own = atoms_ref[...].astype(jnp.float32)
        extended = jnp.concatenate(
            [before[...].astype(jnp.float32), own, after[...].astype(jnp.float32)]
        )
        normed = layer_norm(extended).astype(jnp.bfloat16)
        query, key, value, gate = [
            dot(normed, atom_w_ref[:, m, :]).astype(jnp.bfloat16) for m in range(4)
        ]
        query = query[RIM : RIM + atom_count]
        gate = gate[RIM : RIM + atom_count].astype(jnp.float32)
        factors = pair_w_ref[...].astype(jnp.float32)
        lane = lax.broadcasted_iota(jnp.int32, (QW, CA), 1)
        heads = [
            jnp.logical_and(lane >= h * ATOM_HEAD, lane < (h + 1) * ATOM_HEAD)
            for h in range(ATOM_HEADS)
        ]
        start = (row * peers + col) * atom_count - RIM
        all_atoms = atom_count * peers * rows_n
        spot = lax.broadcasted_iota(jnp.int32, (ATOM_HEADS * QW, KW), 1)
        attended = []
        for window in range(atom_count // QW):
            low = window * QW
            queries = query[low : low + QW].astype(jnp.float32)
            stacked = jnp.concatenate(
                [jnp.where(mask, queries, 0.0) for mask in heads]
            ).astype(jnp.bfloat16)
            planes = [
                atom_pair_ref[window, c].astype(jnp.float32)
                for c in range(atom_pair_ref.shape[1])
            ]
            bias = []
            for h in range(ATOM_HEADS):
                total = planes[0] * factors[h : h + 1, 0:1]
                for c in range(1, len(planes)):
                    total = total + planes[c] * factors[h : h + 1, c : c + 1]
                bias.append(total)
            scores = dot_rows(stacked, key[low : low + KW])
            scores = scores * (1.0 / math.sqrt(ATOM_HEAD)) + jnp.concatenate(bias)
            place = spot + (start + low)
            inside = jnp.logical_and(place >= 0, place < all_atoms)
            weights = softmax_rows(jnp.where(inside, scores, masked_score))
            mixed = dot(weights, value[low : low + KW])
            picked = jnp.where(heads[0], mixed[:QW], 0.0)
            for h in range(1, ATOM_HEADS):
                picked = picked + jnp.where(heads[h], mixed[h * QW : (h + 1) * QW], 0.0)
            attended.append(picked)
        gated = (jax.nn.sigmoid(gate) * jnp.concatenate(attended)).astype(jnp.bfloat16)
        mid_all[col] = (own + dot(gated, atom_wo_ref[...])).astype(jnp.bfloat16)
        for k in range(1, peers):
            to_col(k, mid_all.at[col], mid_all.at[col], mid_s, mid_r).start()

    @pl.when(step == TOKEN_STEP)
    def _():
        for k in range(1, peers):
            to_col(k, token_ref, token_all.at[source(k)], tok_s, tok_r).wait()
            to_col(k, mid_all.at[col], mid_all.at[source(k)], mid_s, mid_r).wait()
        slots = lax.broadcasted_iota(jnp.int32, (query_rows, LANES), 0) + row * query_rows
        counts = jnp.zeros((query_rows, LANES), jnp.float32)
        for c in range(peers):
            match = (slots == token_all[c]).astype(jnp.float32)
            counts = counts + match
            hot[:, c * LANES : (c + 1) * LANES] = match.astype(jnp.bfloat16)
        count = jnp.sum(counts, axis=1, keepdims=True)
        mids = mid_all[...].reshape(peers * atom_count, CA)
        features = jnp.maximum(dot(mids, agg_ref[...]), 0.0).astype(jnp.bfloat16)
        sums = dot(hot[...], features)
        held = (single_ref[...].astype(jnp.float32) + sums * (1.0 / count)).astype(jnp.bfloat16)
        spot = lax.broadcasted_iota(jnp.int32, (held.shape[1], LANES), 0) - col * own_cols
        column = lax.broadcasted_iota(jnp.int32, (held.shape[1], LANES), 1)
        chosen = jnp.logical_and(spot == column, column < own_cols)
        own_in[...] = dot(held, chosen.astype(jnp.float32).astype(jnp.bfloat16)).astype(
            jnp.bfloat16
        )
        normed = layer_norm(held.astype(jnp.float32)).astype(jnp.bfloat16)
        for m in range(4):
            block = dot_rows(normed, token_w_ref[m]).astype(jnp.bfloat16)
            proj[:, m * LANES : m * LANES + own_cols] = block
        kv_all[row] = proj[:, LANES : 3 * LANES]
        for k in range(1, rows_n):
            to_row(k, kv_all.at[row], kv_all.at[row]).start()

    block_steps = BLOCK_ROWS // ROWS_STEP
    blocks = query_rows // BLOCK_ROWS
    near = peers - 1

    def attend(b):
        part_rows = pl.ds(b * BLOCK_ROWS, BLOCK_ROWS)
        if b == 0:
            for k in range(1, rows_n):
                to_row(k, kv_all.at[row], kv_all.at[source_row(k)]).wait()
        for k in range(1, peers):
            to_col(
                k, send.at[pl.ds(other(k) * group, group), part_rows, :],
                bias_all.at[source(k), :, part_rows, :], bias_s, bias_r, b * near,
            ).wait()
        query = proj[part_rows, :LANES].astype(jnp.float32)
        keys = kv_all[:, :, :LANES].reshape(rows_n * query_rows, LANES)
        values = kv_all[:, :, LANES:].reshape(rows_n * query_rows, LANES)
        lane = lax.broadcasted_iota(jnp.int32, (BLOCK_ROWS, LANES), 1)
        masks = [
            jnp.logical_and(lane >= h * HEAD, lane < (h + 1) * HEAD) for h in range(group)
        ]
        stacked = jnp.concatenate([jnp.where(mask, query, 0.0) for mask in masks])
        scores = dot_rows(stacked.astype(jnp.bfloat16), keys) * (1.0 / math.sqrt(HEAD))
        bias = jnp.concatenate(
            [
                jnp.concatenate([bias_all[c, h, part_rows, :] for c in range(peers)], axis=1)
                for h in range(group)
            ]
        )
        mixed = dot(softmax_rows(scores + bias.astype(jnp.float32)), values)
        attended = jnp.where(masks[0], mixed[:BLOCK_ROWS], 0.0)
        for h in range(1, group):
            attended = attended + jnp.where(
                masks[h], mixed[h * BLOCK_ROWS : (h + 1) * BLOCK_ROWS], 0.0
            )
        gate = proj[part_rows, 3 * LANES :].astype(jnp.float32)
        gated = (jax.nn.sigmoid(gate) * attended).astype(jnp.bfloat16)
        part = dot(gated, wo_wide[...]).astype(jnp.bfloat16)
        for c in range(peers):
            part_send[b, c] = part[:, c * LANES : (c + 1) * LANES]
        for k in range(1, peers):
            to_col(
                k, part_send.at[b, other(k)], part_all.at[b, col], part_s, part_r, b * near
            ).start()
        part_all[b, col] = part_send[b, col]

    def finish(b):
        for k in range(1, peers):
            to_col(
                k, part_send.at[b, other(k)], part_all.at[b, source(k)], part_s, part_r, b * near
            ).wait()
        update = part_all[b, 0].astype(jnp.float32)
        for c in range(1, peers):
            update = update + part_all[b, c].astype(jnp.float32)
        part_rows = pl.ds(b * BLOCK_ROWS, BLOCK_ROWS)
        total = own_in[part_rows, :].astype(jnp.float32) + update
        single_rows[part_rows, :] = total.astype(jnp.bfloat16)

    for b, at in enumerate(ATTEND_STEPS):
        pl.when(step == at)(functools.partial(attend, b))

    for b, at in enumerate(FINISH_STEPS):
        pl.when(step == at)(functools.partial(finish, b))

    def first(k):
        x = pair_ref[k * ROWS_CHAIN : (k + 1) * ROWS_CHAIN].reshape(ROWS_CHAIN * width, CZ)
        both = dot_rows(centre_ref[...], x)
        centred = both[:CZ]
        spread = jnp.mean(centred * centred, axis=0, keepdims=True)
        normed = (centred * lax.rsqrt(spread + epsilon)).astype(jnp.bfloat16)
        return centred, both[CZ : CZ + 1], normed

    def second(state):
        centred, average, normed = state
        both = dot(win_ref[...], normed)
        half = both.shape[0] // 2
        gate = both[:half]
        hidden = ((gate + gate * jnp.tanh(gate)) * both[half:]).astype(jnp.bfloat16)
        return centred + average, hidden

    def third(state):
        tile, hidden = state
        update = dot(wout_ref[...], hidden)
        renewed = (tile + update).astype(jnp.bfloat16).astype(jnp.float32)
        centred = renewed - jnp.mean(renewed, axis=0, keepdims=True)
        spread = jnp.mean(centred * centred, axis=0, keepdims=True)
        return (centred * lax.rsqrt(spread + epsilon)).astype(jnp.bfloat16)

    def fourth(k, renormed):
        bias = dot(bw_ref[...], renormed)
        for i in range(ROWS_CHAIN):
            stage[:, k * ROWS_CHAIN + i, :] = bias[:, i * width : (i + 1) * width]

    chains = ROWS_STEP // ROWS_CHAIN
    held = {}
    for turn in range(chains + 3):
        if 0 <= turn - 3:
            fourth(turn - 3, held.pop((2, turn - 3)))
        if 0 <= turn - 2 < chains:
            held[2, turn - 2] = third(held.pop((1, turn - 2)))
        if 0 <= turn - 1 < chains:
            held[1, turn - 1] = second(held.pop((0, turn - 1)))
        if turn < chains:
            held[0, turn] = first(turn)

    rows = pl.ds(pl.multiple_of(step * ROWS_STEP, ROWS_STEP), ROWS_STEP)
    send[:, rows, :] = stage[...].astype(jnp.bfloat16)
    bias_all[col, :, rows, :] = send[pl.ds(col * group, group), rows, :]
    for k in range(1, peers):
        to_col(
            k, send.at[pl.ds(other(k) * group, group), rows, :], bias_all.at[col, :, rows, :],
            bias_s, bias_r, (step // block_steps) * near,
        ).start()

    @pl.when(step == steps - 1)
    def _():
        for b in range(len(FINISH_STEPS), len(ATTEND_STEPS)):
            finish(b)
        for b in range(len(ATTEND_STEPS), blocks):
            attend(b)
        for b in range(len(ATTEND_STEPS), blocks):
            finish(b)
        back = dot_rows(back_t[...], single_rows[...]).astype(jnp.bfloat16)
        picks = dot(back, hot[...]).astype(jnp.bfloat16)
        for c in range(peers):
            pick_send[c] = picks[:, c * LANES : (c + 1) * LANES]
        for k in range(1, peers):
            to_col(k, pick_send.at[other(k)], pick_all.at[col], pick_s, pick_r).start()
        single_out_ref[...] = single_rows[:, :own_cols]
        pick_all[col] = pick_send[col]
        for k in range(1, peers):
            to_col(k, pick_send.at[other(k)], pick_all.at[source(k)], pick_s, pick_r).wait()
        total_back = pick_all[0].astype(jnp.float32)
        for c in range(1, peers):
            total_back = total_back + pick_all[c].astype(jnp.float32)
        total_back = total_back.astype(jnp.bfloat16).astype(jnp.float32).T
        atoms_out_ref[...] = (mid_all[col].astype(jnp.float32) + total_back).astype(jnp.bfloat16)


def body(
    atoms, atom_pair, atom_token, single, pair, atom_w, atom_pair_w, atom_wo, agg_w, trans_in,
    trans_out, bias_w, token_w, token_wo, back_w,
):
    rows, cols, _ = pair.shape
    peers, rows_n = lax.axis_size("col"), lax.axis_size("row")
    heads = bias_w.shape[1]
    hidden = trans_in.shape[2]
    atom_count = atoms.shape[0]
    width = single.shape[1]
    own_cols = token_wo.shape[0]
    bf16 = jnp.bfloat16
    operands = (
        pair, trans_in, trans_out, bias_w.T,
        atoms, atom_pair, atom_token[None, :], single, atom_w, atom_pair_w.T, atom_wo, agg_w,
        token_w.transpose(1, 2, 0), token_wo, back_w,
    )
    whole = lambda value: pl.BlockSpec(value.shape, lambda i, n=value.ndim: (0,) * n)
    in_specs = [pl.BlockSpec((ROWS_STEP, cols, CZ), lambda i: (i, 0, 0))]
    in_specs += [whole(value) for value in operands[1:]]
    dma = lambda n: pltpu.SemaphoreType.DMA((n,))
    p, r = peers - 1, rows_n - 1
    blocks = rows // BLOCK_ROWS
    single_out, atoms_out = pl.pallas_call(
        functools.partial(whole_kernel, peers, rows_n),
        grid=(rows // ROWS_STEP,),
        out_shape=(
            jax.ShapeDtypeStruct((rows, own_cols), bf16),
            jax.ShapeDtypeStruct((atom_count, CA), bf16),
        ),
        in_specs=in_specs,
        out_specs=(
            pl.BlockSpec((rows, own_cols), lambda i: (0, 0)),
            pl.BlockSpec((atom_count, CA), lambda i: (0, 0)),
        ),
        scratch_shapes=[
            pltpu.VMEM((CZ + 16, CZ), bf16),
            pltpu.VMEM((2 * hidden, CZ), bf16),
            pltpu.VMEM((CZ, hidden), bf16),
            pltpu.VMEM((LANES, peers * LANES), bf16),
            pltpu.VMEM((CA, LANES), bf16),
            pltpu.VMEM((rows, LANES), bf16),
            pltpu.VMEM((rows, LANES), bf16),
            pltpu.VMEM((heads, ROWS_STEP, cols), jnp.float32),
            pltpu.VMEM((heads, rows, cols), bf16),
            pltpu.VMEM((peers, heads // peers, rows, cols), bf16),
            pltpu.VMEM((RIM, CA), bf16),
            pltpu.VMEM((RIM, CA), bf16),
            pltpu.VMEM((peers, atom_count, CA), bf16),
            pltpu.VMEM((peers, 1, atom_count), jnp.int32),
            pltpu.VMEM((rows, peers * atom_count), bf16),
            pltpu.VMEM((rows, 4 * LANES), bf16),
            pltpu.VMEM((rows_n, rows, 2 * LANES), bf16),
            pltpu.VMEM((blocks, peers, BLOCK_ROWS, LANES), bf16),
            pltpu.VMEM((blocks, peers, BLOCK_ROWS, LANES), bf16),
            pltpu.VMEM((peers, CA, atom_count), bf16),
            pltpu.VMEM((peers, CA, atom_count), bf16),
            dma(2), dma(2), dma(p), dma(p), dma(p), dma(p), dma(r), dma(r),
            dma(blocks * p), dma(blocks * p), dma(blocks * p), dma(blocks * p), dma(p), dma(p),
        ],
        compiler_params=pltpu.CompilerParams(
            collective_id=0, has_side_effects=True, vmem_limit_bytes=56 * 2**20,
            dimension_semantics=("arbitrary",),
        ),
        cost_estimate=pl.CostEstimate(
            flops=2 * rows * cols * CZ * (3 * hidden + heads + CZ),
            bytes_accessed=2 * rows * cols * (CZ + 2 * heads),
            transcendentals=rows * cols * hidden,
        ),
        name="diffusion_block",
    )(*operands)
    return single_out, atoms_out


def solution(mesh):
    in_specs = (
        P(("row", "col"), None),
        P(("row", "col"), None, None, None),
        P(("row", "col")),
        P("row", None),
        P("row", "col", None),
        P(),
        P(),
        P(),
        P(),
        P(),
        P(),
        P(),
        P(None, None, "col"),
        P("col", None),
        P("col", None),
    )
    out_specs = (P("row", "col"), P(("row", "col"), None))
    return jax.shard_map(body, mesh=mesh, in_specs=in_specs, out_specs=out_specs, check_vma=False)
```

```python
import functools
import math

import jax
import jax.numpy as jnp
from jax import lax
from jax.experimental import pallas as pl
from jax.experimental.pallas import tpu as pltpu
from jax.sharding import PartitionSpec as P

HEADS = 16
HEAD = 48
CA = 128
CZ = 128
ATOM_HEADS = 4
ATOM_HEAD = 32
QW = 32
KW = 128
RIM = (KW - QW) // 2
LANES = 128
ROWS_STEP = 32
ROWS_CHAIN = 8
ATOM_STEP = 2
TOKEN_STEP = 5
MESH = pl.DeviceIdType.MESH


epsilon = 1e-05
masked_score = -1e30


def layer_norm(values):
    centred = values - jnp.mean(values, axis=-1, keepdims=True)
    spread = jnp.mean(centred * centred, axis=-1, keepdims=True)
    return centred * lax.rsqrt(spread + epsilon)


def softmax_rows(scores):
    highest = jnp.max(scores, axis=-1, keepdims=True)
    raised = jnp.exp(scores - highest)
    return (raised * (1.0 / jnp.sum(raised, axis=-1, keepdims=True))).astype(jnp.bfloat16)


def dot(a, b):
    return jnp.dot(a, b, preferred_element_type=jnp.float32)


def dot_rows(a, b):
    return lax.dot_general(a, b, (((1,), (1,)), ((), ())), preferred_element_type=jnp.float32)


def whole_kernel(
    peers, rows_n,
    pair_ref, trans_in_ref, trans_out_ref, bw_ref,
    atoms_ref, atom_pair_ref, token_ref, single_ref, atom_w_ref, pair_w_ref, atom_wo_ref,
    agg_ref, token_w_ref, wo_ref, back_ref,
    single_out_ref, atoms_out_ref,
    centre_ref, win_ref, wout_ref, wo_t, back_t, stage, send, bias_all, before, after, mid_all, token_all, hot, token_in, proj, kv_all,
    part_send, part_all, pick_send, pick_all,
    halo_s, halo_r, tok_s, tok_r, mid_s, mid_r, kv_s, kv_r, bias_s, bias_r,
    part_s, part_r, pick_s, pick_r,
):
    step = pl.program_id(0)
    steps = pl.num_programs(0)
    row, col = lax.axis_index("row"), lax.axis_index("col")
    group = send.shape[0] // peers
    width = pair_ref.shape[1]
    atom_count = atoms_ref.shape[0]
    query_rows = single_ref.shape[0]
    own_cols = back_ref.shape[0]

    def other(k):
        return lax.rem(col + k, peers)

    def source(k):
        return lax.rem(col + peers - k, peers)

    def other_row(k):
        return lax.rem(row + k, rows_n)

    def source_row(k):
        return lax.rem(row + rows_n - k, rows_n)

    def to_col(k, src, dst, s, r):
        return pltpu.make_async_remote_copy(
            src_ref=src, dst_ref=dst, send_sem=s.at[k - 1], recv_sem=r.at[k - 1],
            device_id=(row, other(k)), device_id_type=MESH,
        )

    def to_row(k, src, dst):
        return pltpu.make_async_remote_copy(
            src_ref=src, dst_ref=dst, send_sem=kv_s.at[k - 1], recv_sem=kv_r.at[k - 1],
            device_id=(other_row(k), col), device_id_type=MESH,
        )

    is_first = jnp.logical_and(row == 0, col == 0)
    is_last = jnp.logical_and(row == rows_n - 1, col == peers - 1)
    wraps_up = jnp.logical_and(col == peers - 1, row < rows_n - 1)
    wraps_down = jnp.logical_and(col == 0, row > 0)
    up = (lax.rem(jnp.where(col == peers - 1, row + 1, row), rows_n), lax.rem(col + 1, peers))
    down = (
        lax.rem(jnp.where(col == 0, row + rows_n - 1, row), rows_n),
        lax.rem(col + peers - 1, peers),
    )

    def halo_up():
        return pltpu.make_async_remote_copy(
            src_ref=atoms_ref.at[pl.ds(atom_count - RIM, RIM)], dst_ref=before,
            send_sem=halo_s.at[0], recv_sem=halo_r.at[0], device_id=up, device_id_type=MESH,
        )

    def halo_down():
        return pltpu.make_async_remote_copy(
            src_ref=atoms_ref.at[pl.ds(0, RIM)], dst_ref=after,
            send_sem=halo_s.at[1], recv_sem=halo_r.at[1], device_id=down, device_id_type=MESH,
        )

    @pl.when(step == 0)
    def _():
        barrier = pltpu.get_barrier_semaphore()
        for k in range(1, peers):
            pl.semaphore_signal(barrier, inc=1, device_id=(row, other(k)), device_id_type=MESH)
        for k in range(1, rows_n):
            pl.semaphore_signal(barrier, inc=1, device_id=(other_row(k), col), device_id_type=MESH)

        @pl.when(wraps_up)
        def _():
            pl.semaphore_signal(barrier, inc=1, device_id=up, device_id_type=MESH)

        @pl.when(wraps_down)
        def _():
            pl.semaphore_signal(barrier, inc=1, device_id=down, device_id_type=MESH)

        spots = [lax.broadcasted_iota(jnp.int32, (CZ + 16, CZ), d) for d in (0, 1)]
        mean_part = jnp.where(spots[0] < CZ, -1.0 / CZ, 1.0 / CZ)
        centre_ref[...] = (jnp.where(spots[0] == spots[1], 1.0, 0.0) + mean_part).astype(
            jnp.bfloat16
        )
        half = trans_in_ref.shape[2]
        for m, scale in ((0, 0.5), (1, 1.0)):
            block = trans_in_ref[:, m, :].astype(jnp.float32) * scale
            win_ref[m * half : (m + 1) * half, :] = block.T.astype(jnp.bfloat16)
        wout_ref[...] = trans_out_ref[...].astype(jnp.float32).T.astype(jnp.bfloat16)
        back_t[...] = back_ref[...].astype(jnp.float32).T.astype(jnp.bfloat16)
        wide = jnp.concatenate(
            [
                wo_ref[...].astype(jnp.float32),
                jnp.zeros((LANES - own_cols, wo_ref.shape[1]), jnp.float32),
            ]
        )
        wo_t[...] = wide.T.astype(jnp.bfloat16)
        proj[...] = jnp.zeros_like(proj)

        extra = wraps_up.astype(jnp.int32) + wraps_down.astype(jnp.int32)
        pl.semaphore_wait(barrier, peers + rows_n - 2 + extra)

        @pl.when(jnp.logical_not(is_last))
        def _():
            halo_up().start()

        @pl.when(jnp.logical_not(is_first))
        def _():
            halo_down().start()

        @pl.when(is_first)
        def _():
            before[...] = jnp.zeros_like(before)

        @pl.when(is_last)
        def _():
            after[...] = jnp.zeros_like(after)

        token_all[col] = token_ref[...]
        for k in range(1, peers):
            to_col(k, token_ref, token_all.at[col], tok_s, tok_r).start()

    @pl.when(step == ATOM_STEP)
    def _():
        @pl.when(jnp.logical_not(is_last))
        def _():
            halo_up().wait_send()
            halo_down().wait_recv()

        @pl.when(jnp.logical_not(is_first))
        def _():
            halo_down().wait_send()
            halo_up().wait_recv()

        own = atoms_ref[...].astype(jnp.float32)
        extended = jnp.concatenate(
            [before[...].astype(jnp.float32), own, after[...].astype(jnp.float32)]
        )
        normed = layer_norm(extended).astype(jnp.bfloat16)
        query, key, value, gate = [
            dot(normed, atom_w_ref[:, m, :]).astype(jnp.bfloat16) for m in range(4)
        ]
        query = query[RIM : RIM + atom_count]
        gate = gate[RIM : RIM + atom_count].astype(jnp.float32)
        factors = pair_w_ref[...].astype(jnp.float32)
        lane = lax.broadcasted_iota(jnp.int32, (QW, CA), 1)
        heads = [
            jnp.logical_and(lane >= h * ATOM_HEAD, lane < (h + 1) * ATOM_HEAD)
            for h in range(ATOM_HEADS)
        ]
        start = (row * peers + col) * atom_count - RIM
        all_atoms = atom_count * peers * rows_n
        spot = lax.broadcasted_iota(jnp.int32, (ATOM_HEADS * QW, KW), 1)
        attended = []
        for window in range(atom_count // QW):
            low = window * QW
            queries = query[low : low + QW].astype(jnp.float32)
            stacked = jnp.concatenate(
                [jnp.where(mask, queries, 0.0) for mask in heads]
            ).astype(jnp.bfloat16)
            planes = [
                atom_pair_ref[window, c].astype(jnp.float32)
                for c in range(atom_pair_ref.shape[1])
            ]
            bias = []
            for h in range(ATOM_HEADS):
                total = planes[0] * factors[h : h + 1, 0:1]
                for c in range(1, len(planes)):
                    total = total + planes[c] * factors[h : h + 1, c : c + 1]
                bias.append(total)
            scores = dot_rows(stacked, key[low : low + KW])
            scores = scores * (1.0 / math.sqrt(ATOM_HEAD)) + jnp.concatenate(bias)
            place = spot + (start + low)
            inside = jnp.logical_and(place >= 0, place < all_atoms)
            weights = softmax_rows(jnp.where(inside, scores, masked_score))
            mixed = dot(weights, value[low : low + KW])
            picked = jnp.where(heads[0], mixed[:QW], 0.0)
            for h in range(1, ATOM_HEADS):
                picked = picked + jnp.where(heads[h], mixed[h * QW : (h + 1) * QW], 0.0)
            attended.append(picked)
        gated = (jax.nn.sigmoid(gate) * jnp.concatenate(attended)).astype(jnp.bfloat16)
        mid_all[col] = (own + dot(gated, atom_wo_ref[...])).astype(jnp.bfloat16)
        for k in range(1, peers):
            to_col(k, mid_all.at[col], mid_all.at[col], mid_s, mid_r).start()

    @pl.when(step == TOKEN_STEP)
    def _():
        for k in range(1, peers):
            to_col(k, token_ref, token_all.at[source(k)], tok_s, tok_r).wait()
            to_col(k, mid_all.at[col], mid_all.at[source(k)], mid_s, mid_r).wait()
        slots = lax.broadcasted_iota(jnp.int32, (query_rows, LANES), 0) + row * query_rows
        counts = jnp.zeros((query_rows, LANES), jnp.float32)
        for c in range(peers):
            match = (slots == token_all[c]).astype(jnp.float32)
            counts = counts + match
            hot[:, c * LANES : (c + 1) * LANES] = match.astype(jnp.bfloat16)
        count = jnp.sum(counts, axis=1, keepdims=True)
        mids = mid_all[...].reshape(peers * atom_count, CA)
        features = jnp.maximum(dot(mids, agg_ref[...]), 0.0).astype(jnp.bfloat16)
        sums = dot(hot[...], features)
        held = (single_ref[...].astype(jnp.float32) + sums * (1.0 / count)).astype(jnp.bfloat16)
        token_in[...] = held
        normed = layer_norm(held.astype(jnp.float32)).astype(jnp.bfloat16)
        for m in range(4):
            block = dot_rows(normed, token_w_ref[m]).astype(jnp.bfloat16)
            proj[:, m * LANES : m * LANES + own_cols] = block
        kv_all[row] = proj[:, LANES : 3 * LANES]
        for k in range(1, rows_n):
            to_row(k, kv_all.at[row], kv_all.at[row]).start()

    def first(k):
        x = pair_ref[k * ROWS_CHAIN : (k + 1) * ROWS_CHAIN].reshape(ROWS_CHAIN * width, CZ)
        both = dot_rows(centre_ref[...], x)
        centred = both[:CZ]
        spread = jnp.mean(centred * centred, axis=0, keepdims=True)
        normed = (centred * lax.rsqrt(spread + epsilon)).astype(jnp.bfloat16)
        return centred, both[CZ : CZ + 1], normed

    def second(state):
        centred, average, normed = state
        both = dot(win_ref[...], normed)
        half = both.shape[0] // 2
        gate = both[:half]
        hidden = ((gate + gate * jnp.tanh(gate)) * both[half:]).astype(jnp.bfloat16)
        return centred + average, hidden

    def third(state):
        tile, hidden = state
        update = dot(wout_ref[...], hidden)
        renewed = (tile + update).astype(jnp.bfloat16).astype(jnp.float32)
        centred = renewed - jnp.mean(renewed, axis=0, keepdims=True)
        spread = jnp.mean(centred * centred, axis=0, keepdims=True)
        return (centred * lax.rsqrt(spread + epsilon)).astype(jnp.bfloat16)

    def fourth(k, renormed):
        bias = dot(bw_ref[...], renormed)
        for i in range(ROWS_CHAIN):
            stage[:, k * ROWS_CHAIN + i, :] = bias[:, i * width : (i + 1) * width]

    chains = ROWS_STEP // ROWS_CHAIN
    held = {}
    for turn in range(chains + 3):
        if 0 <= turn - 3:
            fourth(turn - 3, held.pop((2, turn - 3)))
        if 0 <= turn - 2 < chains:
            held[2, turn - 2] = third(held.pop((1, turn - 2)))
        if 0 <= turn - 1 < chains:
            held[1, turn - 1] = second(held.pop((0, turn - 1)))
        if turn < chains:
            held[0, turn] = first(turn)

    rows = pl.ds(pl.multiple_of(step * ROWS_STEP, ROWS_STEP), ROWS_STEP)
    send[:, rows, :] = stage[...].astype(jnp.bfloat16)
    bias_all[col, :, rows, :] = send[pl.ds(col * group, group), rows, :]
    for k in range(1, peers):
        to_col(
            k, send.at[pl.ds(other(k) * group, group), rows, :], bias_all.at[col, :, rows, :],
            bias_s, bias_r,
        ).start()

    @pl.when(step == steps - 1)
    def _():
        for k in range(1, rows_n):
            to_row(k, kv_all.at[row], kv_all.at[source_row(k)]).wait()
        for k in range(1, peers):
            to_col(
                k, send.at[pl.ds(other(k) * group, group)], bias_all.at[source(k)], bias_s, bias_r
            ).wait()
        query = proj[:, :LANES].astype(jnp.float32)
        keys = kv_all[:, :, :LANES].reshape(rows_n * query_rows, LANES)
        values = kv_all[:, :, LANES:].reshape(rows_n * query_rows, LANES)
        lane = lax.broadcasted_iota(jnp.int32, (query_rows, LANES), 1)
        attended = jnp.zeros((query_rows, LANES), jnp.float32)
        for h in range(group):
            mask = jnp.logical_and(lane >= h * HEAD, lane < (h + 1) * HEAD)
            scores = dot_rows(jnp.where(mask, query, 0.0).astype(jnp.bfloat16), keys)
            bias = jnp.concatenate([bias_all[c, h] for c in range(peers)], axis=1)
            weights = softmax_rows(scores * (1.0 / math.sqrt(HEAD)) + bias.astype(jnp.float32))
            attended = attended + jnp.where(mask, dot(weights, values), 0.0)
        gate = proj[:, 3 * LANES :].astype(jnp.float32)
        gated = (jax.nn.sigmoid(gate) * attended).astype(jnp.bfloat16)
        part = dot_rows(wo_t[...], gated).astype(jnp.bfloat16)
        part_send[...] = part.reshape(peers, own_cols, query_rows)
        for k in range(1, peers):
            to_col(k, part_send.at[other(k)], part_all.at[col], part_s, part_r).start()
        spot = lax.broadcasted_iota(jnp.int32, (own_cols, token_in.shape[1]), 0) + col * own_cols
        column = lax.broadcasted_iota(jnp.int32, (own_cols, token_in.shape[1]), 1)
        chosen = (spot == column).astype(jnp.float32).astype(jnp.bfloat16)
        total = dot_rows(chosen, token_in[...])
        part_all[col] = part_send[col]
        for k in range(1, peers):
            to_col(k, part_send.at[other(k)], part_all.at[source(k)], part_s, part_r).wait()
        update = part_all[0].astype(jnp.float32)
        for c in range(1, peers):
            update = update + part_all[c].astype(jnp.float32)
        fresh = total + update
        single_t = fresh.astype(jnp.bfloat16)
        back = dot(back_t[...], single_t).astype(jnp.bfloat16)
        picks = dot(back, hot[...]).astype(jnp.bfloat16)
        for c in range(peers):
            pick_send[c] = picks[:, c * LANES : (c + 1) * LANES]
        for k in range(1, peers):
            to_col(k, pick_send.at[other(k)], pick_all.at[col], pick_s, pick_r).start()
        single_out_ref[...] = single_t
        pick_all[col] = pick_send[col]
        for k in range(1, peers):
            to_col(k, pick_send.at[other(k)], pick_all.at[source(k)], pick_s, pick_r).wait()
        total_back = pick_all[0].astype(jnp.float32)
        for c in range(1, peers):
            total_back = total_back + pick_all[c].astype(jnp.float32)
        total_back = total_back.astype(jnp.bfloat16).astype(jnp.float32).T
        atoms_out_ref[...] = (mid_all[col].astype(jnp.float32) + total_back).astype(jnp.bfloat16)


def body(
    atoms, atom_pair, atom_token, single, pair, atom_w, atom_pair_w, atom_wo, agg_w, trans_in,
    trans_out, bias_w, token_w, token_wo, back_w,
):
    rows, cols, _ = pair.shape
    peers, rows_n = lax.axis_size("col"), lax.axis_size("row")
    heads = bias_w.shape[1]
    hidden = trans_in.shape[2]
    atom_count = atoms.shape[0]
    width = single.shape[1]
    own_cols = token_wo.shape[0]
    bf16 = jnp.bfloat16
    operands = (
        pair, trans_in, trans_out, bias_w.T,
        atoms, atom_pair, atom_token[None, :], single, atom_w, atom_pair_w.T, atom_wo, agg_w,
        token_w.transpose(1, 2, 0), token_wo, back_w,
    )
    whole = lambda value: pl.BlockSpec(value.shape, lambda i, n=value.ndim: (0,) * n)
    in_specs = [pl.BlockSpec((ROWS_STEP, cols, CZ), lambda i: (i, 0, 0))]
    in_specs += [whole(value) for value in operands[1:]]
    dma = lambda n: pltpu.SemaphoreType.DMA((n,))
    p, r = peers - 1, rows_n - 1
    single_out, atoms_out = pl.pallas_call(
        functools.partial(whole_kernel, peers, rows_n),
        grid=(rows // ROWS_STEP,),
        out_shape=(
            jax.ShapeDtypeStruct((own_cols, rows), bf16),
            jax.ShapeDtypeStruct((atom_count, CA), bf16),
        ),
        in_specs=in_specs,
        out_specs=(
            pl.BlockSpec((own_cols, rows), lambda i: (0, 0)),
            pl.BlockSpec((atom_count, CA), lambda i: (0, 0)),
        ),
        scratch_shapes=[
            pltpu.VMEM((CZ + 16, CZ), bf16),
            pltpu.VMEM((2 * hidden, CZ), bf16),
            pltpu.VMEM((CZ, hidden), bf16),
            pltpu.VMEM((width, LANES), bf16),
            pltpu.VMEM((CA, own_cols), bf16),
            pltpu.VMEM((heads, ROWS_STEP, cols), jnp.float32),
            pltpu.VMEM((heads, rows, cols), bf16),
            pltpu.VMEM((peers, heads // peers, rows, cols), bf16),
            pltpu.VMEM((RIM, CA), bf16),
            pltpu.VMEM((RIM, CA), bf16),
            pltpu.VMEM((peers, atom_count, CA), bf16),
            pltpu.VMEM((peers, 1, atom_count), jnp.int32),
            pltpu.VMEM((rows, peers * atom_count), bf16),
            pltpu.VMEM((rows, width), bf16),
            pltpu.VMEM((rows, 4 * LANES), bf16),
            pltpu.VMEM((rows_n, rows, 2 * LANES), bf16),
            pltpu.VMEM((peers, own_cols, rows), bf16),
            pltpu.VMEM((peers, own_cols, rows), bf16),
            pltpu.VMEM((peers, CA, atom_count), bf16),
            pltpu.VMEM((peers, CA, atom_count), bf16),
            dma(2), dma(2), dma(p), dma(p), dma(p), dma(p), dma(r), dma(r), dma(p), dma(p),
            dma(p), dma(p), dma(p), dma(p),
        ],
        compiler_params=pltpu.CompilerParams(
            collective_id=0, has_side_effects=True, vmem_limit_bytes=56 * 2**20,
            dimension_semantics=("arbitrary",),
        ),
        cost_estimate=pl.CostEstimate(
            flops=2 * rows * cols * CZ * (3 * hidden + heads + CZ),
            bytes_accessed=2 * rows * cols * (CZ + 2 * heads),
            transcendentals=rows * cols * hidden,
        ),
        name="diffusion_block",
    )(*operands)
    return single_out.T, atoms_out


def solution(mesh):
    in_specs = (
        P(("row", "col"), None),
        P(("row", "col"), None, None, None),
        P(("row", "col")),
        P("row", None),
        P("row", "col", None),
        P(),
        P(),
        P(),
        P(),
        P(),
        P(),
        P(),
        P(None, None, "col"),
        P("col", None),
        P("col", None),
    )
    out_specs = (P("row", "col"), P(("row", "col"), None))
    return jax.shard_map(body, mesh=mesh, in_specs=in_specs, out_specs=out_specs, check_vma=False)
```

```python
import functools
import math

import jax
import jax.numpy as jnp
from jax import lax
from jax.experimental import pallas as pl
from jax.experimental.pallas import tpu as pltpu
from jax.sharding import PartitionSpec as P

HEADS = 16
HEAD = 48
CA = 128
CZ = 128
ATOM_HEADS = 4
ATOM_HEAD = 32
QW = 32
KW = 128
RIM = (KW - QW) // 2
LANES = 128
ROWS_STEP = 32
ROWS_CHAIN = 8
ATOM_STEP = 2
TOKEN_STEP = 5
BLOCK_ROWS = 128
MESH = pl.DeviceIdType.MESH


epsilon = 1e-05
masked_score = -1e30


def layer_norm(values):
    centred = values - jnp.mean(values, axis=-1, keepdims=True)
    spread = jnp.mean(centred * centred, axis=-1, keepdims=True)
    return centred * lax.rsqrt(spread + epsilon)


def softmax_rows(scores):
    highest = jnp.max(scores, axis=-1, keepdims=True)
    raised = jnp.exp(scores - highest)
    return (raised * (1.0 / jnp.sum(raised, axis=-1, keepdims=True))).astype(jnp.bfloat16)


def dot(a, b):
    return jnp.dot(a, b, preferred_element_type=jnp.float32)


def dot_rows(a, b):
    return lax.dot_general(a, b, (((1,), (1,)), ((), ())), preferred_element_type=jnp.float32)


def whole_kernel(
    peers, rows_n,
    pair_ref, trans_in_ref, trans_out_ref, bw_ref,
    atoms_ref, atom_pair_ref, token_ref, single_ref, atom_w_ref, pair_w_ref, atom_wo_ref,
    agg_ref, token_w_ref, wo_ref, back_ref,
    single_out_ref, atoms_out_ref,
    centre_ref, win_ref, wout_ref, wo_t, back_t, stage, send, bias_all, before, after, mid_all, token_all, hot, token_in, proj, kv_all,
    part_send, part_all, pick_send, pick_all,
    halo_s, halo_r, tok_s, tok_r, mid_s, mid_r, kv_s, kv_r, bias_s, bias_r,
    part_s, part_r, pick_s, pick_r,
):
    step = pl.program_id(0)
    steps = pl.num_programs(0)
    row, col = lax.axis_index("row"), lax.axis_index("col")
    group = send.shape[0] // peers
    width = pair_ref.shape[1]
    atom_count = atoms_ref.shape[0]
    query_rows = single_ref.shape[0]
    own_cols = back_ref.shape[0]

    def other(k):
        return lax.rem(col + k, peers)

    def source(k):
        return lax.rem(col + peers - k, peers)

    def other_row(k):
        return lax.rem(row + k, rows_n)

    def source_row(k):
        return lax.rem(row + rows_n - k, rows_n)

    def to_col(k, src, dst, s, r, base=0):
        return pltpu.make_async_remote_copy(
            src_ref=src, dst_ref=dst, send_sem=s.at[base + k - 1],
            recv_sem=r.at[base + k - 1], device_id=(row, other(k)), device_id_type=MESH,
        )

    def to_row(k, src, dst):
        return pltpu.make_async_remote_copy(
            src_ref=src, dst_ref=dst, send_sem=kv_s.at[k - 1], recv_sem=kv_r.at[k - 1],
            device_id=(other_row(k), col), device_id_type=MESH,
        )

    is_first = jnp.logical_and(row == 0, col == 0)
    is_last = jnp.logical_and(row == rows_n - 1, col == peers - 1)
    wraps_up = jnp.logical_and(col == peers - 1, row < rows_n - 1)
    wraps_down = jnp.logical_and(col == 0, row > 0)
    up = (lax.rem(jnp.where(col == peers - 1, row + 1, row), rows_n), lax.rem(col + 1, peers))
    down = (
        lax.rem(jnp.where(col == 0, row + rows_n - 1, row), rows_n),
        lax.rem(col + peers - 1, peers),
    )

    def halo_up():
        return pltpu.make_async_remote_copy(
            src_ref=atoms_ref.at[pl.ds(atom_count - RIM, RIM)], dst_ref=before,
            send_sem=halo_s.at[0], recv_sem=halo_r.at[0], device_id=up, device_id_type=MESH,
        )

    def halo_down():
        return pltpu.make_async_remote_copy(
            src_ref=atoms_ref.at[pl.ds(0, RIM)], dst_ref=after,
            send_sem=halo_s.at[1], recv_sem=halo_r.at[1], device_id=down, device_id_type=MESH,
        )

    @pl.when(step == 0)
    def _():
        barrier = pltpu.get_barrier_semaphore()
        for k in range(1, peers):
            pl.semaphore_signal(barrier, inc=1, device_id=(row, other(k)), device_id_type=MESH)
        for k in range(1, rows_n):
            pl.semaphore_signal(barrier, inc=1, device_id=(other_row(k), col), device_id_type=MESH)

        @pl.when(wraps_up)
        def _():
            pl.semaphore_signal(barrier, inc=1, device_id=up, device_id_type=MESH)

        @pl.when(wraps_down)
        def _():
            pl.semaphore_signal(barrier, inc=1, device_id=down, device_id_type=MESH)

        spots = [lax.broadcasted_iota(jnp.int32, (CZ + 16, CZ), d) for d in (0, 1)]
        mean_part = jnp.where(spots[0] < CZ, -1.0 / CZ, 1.0 / CZ)
        centre_ref[...] = (jnp.where(spots[0] == spots[1], 1.0, 0.0) + mean_part).astype(
            jnp.bfloat16
        )
        half = trans_in_ref.shape[2]
        for m, scale in ((0, 0.5), (1, 1.0)):
            block = trans_in_ref[:, m, :].astype(jnp.float32) * scale
            win_ref[m * half : (m + 1) * half, :] = block.T.astype(jnp.bfloat16)
        wout_ref[...] = trans_out_ref[...].astype(jnp.float32).T.astype(jnp.bfloat16)
        back_t[...] = back_ref[...].astype(jnp.float32).T.astype(jnp.bfloat16)
        wide = jnp.concatenate(
            [
                wo_ref[...].astype(jnp.float32),
                jnp.zeros((LANES - own_cols, wo_ref.shape[1]), jnp.float32),
            ]
        )
        wo_t[...] = wide.T.astype(jnp.bfloat16)
        proj[...] = jnp.zeros_like(proj)

        extra = wraps_up.astype(jnp.int32) + wraps_down.astype(jnp.int32)
        pl.semaphore_wait(barrier, peers + rows_n - 2 + extra)

        @pl.when(jnp.logical_not(is_last))
        def _():
            halo_up().start()

        @pl.when(jnp.logical_not(is_first))
        def _():
            halo_down().start()

        @pl.when(is_first)
        def _():
            before[...] = jnp.zeros_like(before)

        @pl.when(is_last)
        def _():
            after[...] = jnp.zeros_like(after)

        token_all[col] = token_ref[...]
        for k in range(1, peers):
            to_col(k, token_ref, token_all.at[col], tok_s, tok_r).start()

    @pl.when(step == ATOM_STEP)
    def _():
        @pl.when(jnp.logical_not(is_last))
        def _():
            halo_up().wait_send()
            halo_down().wait_recv()

        @pl.when(jnp.logical_not(is_first))
        def _():
            halo_down().wait_send()
            halo_up().wait_recv()

        own = atoms_ref[...].astype(jnp.float32)
        extended = jnp.concatenate(
            [before[...].astype(jnp.float32), own, after[...].astype(jnp.float32)]
        )
        normed = layer_norm(extended).astype(jnp.bfloat16)
        query, key, value, gate = [
            dot(normed, atom_w_ref[:, m, :]).astype(jnp.bfloat16) for m in range(4)
        ]
        query = query[RIM : RIM + atom_count]
        gate = gate[RIM : RIM + atom_count].astype(jnp.float32)
        factors = pair_w_ref[...].astype(jnp.float32)
        lane = lax.broadcasted_iota(jnp.int32, (QW, CA), 1)
        heads = [
            jnp.logical_and(lane >= h * ATOM_HEAD, lane < (h + 1) * ATOM_HEAD)
            for h in range(ATOM_HEADS)
        ]
        start = (row * peers + col) * atom_count - RIM
        all_atoms = atom_count * peers * rows_n
        spot = lax.broadcasted_iota(jnp.int32, (ATOM_HEADS * QW, KW), 1)
        attended = []
        for window in range(atom_count // QW):
            low = window * QW
            queries = query[low : low + QW].astype(jnp.float32)
            stacked = jnp.concatenate(
                [jnp.where(mask, queries, 0.0) for mask in heads]
            ).astype(jnp.bfloat16)
            planes = [
                atom_pair_ref[window, c].astype(jnp.float32)
                for c in range(atom_pair_ref.shape[1])
            ]
            bias = []
            for h in range(ATOM_HEADS):
                total = planes[0] * factors[h : h + 1, 0:1]
                for c in range(1, len(planes)):
                    total = total + planes[c] * factors[h : h + 1, c : c + 1]
                bias.append(total)
            scores = dot_rows(stacked, key[low : low + KW])
            scores = scores * (1.0 / math.sqrt(ATOM_HEAD)) + jnp.concatenate(bias)
            place = spot + (start + low)
            inside = jnp.logical_and(place >= 0, place < all_atoms)
            weights = softmax_rows(jnp.where(inside, scores, masked_score))
            mixed = dot(weights, value[low : low + KW])
            picked = jnp.where(heads[0], mixed[:QW], 0.0)
            for h in range(1, ATOM_HEADS):
                picked = picked + jnp.where(heads[h], mixed[h * QW : (h + 1) * QW], 0.0)
            attended.append(picked)
        gated = (jax.nn.sigmoid(gate) * jnp.concatenate(attended)).astype(jnp.bfloat16)
        mid_all[col] = (own + dot(gated, atom_wo_ref[...])).astype(jnp.bfloat16)
        for k in range(1, peers):
            to_col(k, mid_all.at[col], mid_all.at[col], mid_s, mid_r).start()

    @pl.when(step == TOKEN_STEP)
    def _():
        for k in range(1, peers):
            to_col(k, token_ref, token_all.at[source(k)], tok_s, tok_r).wait()
            to_col(k, mid_all.at[col], mid_all.at[source(k)], mid_s, mid_r).wait()
        slots = lax.broadcasted_iota(jnp.int32, (query_rows, LANES), 0) + row * query_rows
        counts = jnp.zeros((query_rows, LANES), jnp.float32)
        for c in range(peers):
            match = (slots == token_all[c]).astype(jnp.float32)
            counts = counts + match
            hot[:, c * LANES : (c + 1) * LANES] = match.astype(jnp.bfloat16)
        count = jnp.sum(counts, axis=1, keepdims=True)
        mids = mid_all[...].reshape(peers * atom_count, CA)
        features = jnp.maximum(dot(mids, agg_ref[...]), 0.0).astype(jnp.bfloat16)
        sums = dot(hot[...], features)
        held = (single_ref[...].astype(jnp.float32) + sums * (1.0 / count)).astype(jnp.bfloat16)
        token_in[...] = held
        normed = layer_norm(held.astype(jnp.float32)).astype(jnp.bfloat16)
        for m in range(4):
            block = dot_rows(normed, token_w_ref[m]).astype(jnp.bfloat16)
            proj[:, m * LANES : m * LANES + own_cols] = block
        kv_all[row] = proj[:, LANES : 3 * LANES]
        for k in range(1, rows_n):
            to_row(k, kv_all.at[row], kv_all.at[row]).start()

    block_steps = BLOCK_ROWS // ROWS_STEP
    blocks = query_rows // BLOCK_ROWS
    near = peers - 1

    def attend(b):
        part_rows = pl.ds(b * BLOCK_ROWS, BLOCK_ROWS)
        for k in range(1, peers):
            to_col(
                k, send.at[pl.ds(other(k) * group, group), part_rows, :],
                bias_all.at[source(k), :, part_rows, :], bias_s, bias_r, b * near,
            ).wait()
        query = proj[part_rows, :LANES].astype(jnp.float32)
        keys = kv_all[:, :, :LANES].reshape(rows_n * query_rows, LANES)
        values = kv_all[:, :, LANES:].reshape(rows_n * query_rows, LANES)
        lane = lax.broadcasted_iota(jnp.int32, (BLOCK_ROWS, LANES), 1)
        masks = [
            jnp.logical_and(lane >= h * HEAD, lane < (h + 1) * HEAD) for h in range(group)
        ]
        stacked = jnp.concatenate([jnp.where(mask, query, 0.0) for mask in masks])
        scores = dot_rows(stacked.astype(jnp.bfloat16), keys) * (1.0 / math.sqrt(HEAD))
        bias = jnp.concatenate(
            [
                jnp.concatenate([bias_all[c, h, part_rows, :] for c in range(peers)], axis=1)
                for h in range(group)
            ]
        )
        mixed = dot(softmax_rows(scores + bias.astype(jnp.float32)), values)
        attended = jnp.where(masks[0], mixed[:BLOCK_ROWS], 0.0)
        for h in range(1, group):
            attended = attended + jnp.where(
                masks[h], mixed[h * BLOCK_ROWS : (h + 1) * BLOCK_ROWS], 0.0
            )
        gate = proj[part_rows, 3 * LANES :].astype(jnp.float32)
        gated = (jax.nn.sigmoid(gate) * attended).astype(jnp.bfloat16)
        part = dot_rows(wo_t[...], gated).astype(jnp.bfloat16)
        part_send[b] = part.reshape(peers, own_cols, BLOCK_ROWS)
        for k in range(1, peers):
            to_col(
                k, part_send.at[b, other(k)], part_all.at[b, col], part_s, part_r, b * near
            ).start()
        part_all[b, col] = part_send[b, col]

    def summed(b):
        for k in range(1, peers):
            to_col(
                k, part_send.at[b, other(k)], part_all.at[b, source(k)], part_s, part_r, b * near
            ).wait()
        update = part_all[b, 0].astype(jnp.float32)
        for c in range(1, peers):
            update = update + part_all[b, c].astype(jnp.float32)
        return update

    def first(k):
        x = pair_ref[k * ROWS_CHAIN : (k + 1) * ROWS_CHAIN].reshape(ROWS_CHAIN * width, CZ)
        both = dot_rows(centre_ref[...], x)
        centred = both[:CZ]
        spread = jnp.mean(centred * centred, axis=0, keepdims=True)
        normed = (centred * lax.rsqrt(spread + epsilon)).astype(jnp.bfloat16)
        return centred, both[CZ : CZ + 1], normed

    def second(state):
        centred, average, normed = state
        both = dot(win_ref[...], normed)
        half = both.shape[0] // 2
        gate = both[:half]
        hidden = ((gate + gate * jnp.tanh(gate)) * both[half:]).astype(jnp.bfloat16)
        return centred + average, hidden

    def third(state):
        tile, hidden = state
        update = dot(wout_ref[...], hidden)
        renewed = (tile + update).astype(jnp.bfloat16).astype(jnp.float32)
        centred = renewed - jnp.mean(renewed, axis=0, keepdims=True)
        spread = jnp.mean(centred * centred, axis=0, keepdims=True)
        return (centred * lax.rsqrt(spread + epsilon)).astype(jnp.bfloat16)

    def fourth(k, renormed):
        bias = dot(bw_ref[...], renormed)
        for i in range(ROWS_CHAIN):
            stage[:, k * ROWS_CHAIN + i, :] = bias[:, i * width : (i + 1) * width]

    chains = ROWS_STEP // ROWS_CHAIN
    held = {}
    for turn in range(chains + 3):
        if 0 <= turn - 3:
            fourth(turn - 3, held.pop((2, turn - 3)))
        if 0 <= turn - 2 < chains:
            held[2, turn - 2] = third(held.pop((1, turn - 2)))
        if 0 <= turn - 1 < chains:
            held[1, turn - 1] = second(held.pop((0, turn - 1)))
        if turn < chains:
            held[0, turn] = first(turn)

    rows = pl.ds(pl.multiple_of(step * ROWS_STEP, ROWS_STEP), ROWS_STEP)
    send[:, rows, :] = stage[...].astype(jnp.bfloat16)
    bias_all[col, :, rows, :] = send[pl.ds(col * group, group), rows, :]
    for k in range(1, peers):
        to_col(
            k, send.at[pl.ds(other(k) * group, group), rows, :], bias_all.at[col, :, rows, :],
            bias_s, bias_r, (step // block_steps) * near,
        ).start()

    @pl.when(step == steps - 1)
    def _():
        for k in range(1, rows_n):
            to_row(k, kv_all.at[row], kv_all.at[source_row(k)]).wait()
        for b in range(blocks):
            attend(b)
        spot = lax.broadcasted_iota(jnp.int32, (own_cols, token_in.shape[1]), 0) + col * own_cols
        column = lax.broadcasted_iota(jnp.int32, (own_cols, token_in.shape[1]), 1)
        chosen = (spot == column).astype(jnp.float32).astype(jnp.bfloat16)
        total = dot_rows(chosen, token_in[...])
        update = jnp.concatenate([summed(b) for b in range(blocks)], axis=1)
        fresh = total + update
        single_t = fresh.astype(jnp.bfloat16)
        back = dot(back_t[...], single_t).astype(jnp.bfloat16)
        picks = dot(back, hot[...]).astype(jnp.bfloat16)
        for c in range(peers):
            pick_send[c] = picks[:, c * LANES : (c + 1) * LANES]
        for k in range(1, peers):
            to_col(k, pick_send.at[other(k)], pick_all.at[col], pick_s, pick_r).start()
        single_out_ref[...] = single_t
        pick_all[col] = pick_send[col]
        for k in range(1, peers):
            to_col(k, pick_send.at[other(k)], pick_all.at[source(k)], pick_s, pick_r).wait()
        total_back = pick_all[0].astype(jnp.float32)
        for c in range(1, peers):
            total_back = total_back + pick_all[c].astype(jnp.float32)
        total_back = total_back.astype(jnp.bfloat16).astype(jnp.float32).T
        atoms_out_ref[...] = (mid_all[col].astype(jnp.float32) + total_back).astype(jnp.bfloat16)


def body(
    atoms, atom_pair, atom_token, single, pair, atom_w, atom_pair_w, atom_wo, agg_w, trans_in,
    trans_out, bias_w, token_w, token_wo, back_w,
):
    rows, cols, _ = pair.shape
    peers, rows_n = lax.axis_size("col"), lax.axis_size("row")
    heads = bias_w.shape[1]
    hidden = trans_in.shape[2]
    atom_count = atoms.shape[0]
    width = single.shape[1]
    own_cols = token_wo.shape[0]
    bf16 = jnp.bfloat16
    operands = (
        pair, trans_in, trans_out, bias_w.T,
        atoms, atom_pair, atom_token[None, :], single, atom_w, atom_pair_w.T, atom_wo, agg_w,
        token_w.transpose(1, 2, 0), token_wo, back_w,
    )
    whole = lambda value: pl.BlockSpec(value.shape, lambda i, n=value.ndim: (0,) * n)
    in_specs = [pl.BlockSpec((ROWS_STEP, cols, CZ), lambda i: (i, 0, 0))]
    in_specs += [whole(value) for value in operands[1:]]
    dma = lambda n: pltpu.SemaphoreType.DMA((n,))
    p, r = peers - 1, rows_n - 1
    blocks = rows // BLOCK_ROWS
    single_out, atoms_out = pl.pallas_call(
        functools.partial(whole_kernel, peers, rows_n),
        grid=(rows // ROWS_STEP,),
        out_shape=(
            jax.ShapeDtypeStruct((own_cols, rows), bf16),
            jax.ShapeDtypeStruct((atom_count, CA), bf16),
        ),
        in_specs=in_specs,
        out_specs=(
            pl.BlockSpec((own_cols, rows), lambda i: (0, 0)),
            pl.BlockSpec((atom_count, CA), lambda i: (0, 0)),
        ),
        scratch_shapes=[
            pltpu.VMEM((CZ + 16, CZ), bf16),
            pltpu.VMEM((2 * hidden, CZ), bf16),
            pltpu.VMEM((CZ, hidden), bf16),
            pltpu.VMEM((width, LANES), bf16),
            pltpu.VMEM((CA, own_cols), bf16),
            pltpu.VMEM((heads, ROWS_STEP, cols), jnp.float32),
            pltpu.VMEM((heads, rows, cols), bf16),
            pltpu.VMEM((peers, heads // peers, rows, cols), bf16),
            pltpu.VMEM((RIM, CA), bf16),
            pltpu.VMEM((RIM, CA), bf16),
            pltpu.VMEM((peers, atom_count, CA), bf16),
            pltpu.VMEM((peers, 1, atom_count), jnp.int32),
            pltpu.VMEM((rows, peers * atom_count), bf16),
            pltpu.VMEM((rows, width), bf16),
            pltpu.VMEM((rows, 4 * LANES), bf16),
            pltpu.VMEM((rows_n, rows, 2 * LANES), bf16),
            pltpu.VMEM((blocks, peers, own_cols, BLOCK_ROWS), bf16),
            pltpu.VMEM((blocks, peers, own_cols, BLOCK_ROWS), bf16),
            pltpu.VMEM((peers, CA, atom_count), bf16),
            pltpu.VMEM((peers, CA, atom_count), bf16),
            dma(2), dma(2), dma(p), dma(p), dma(p), dma(p), dma(r), dma(r),
            dma(blocks * p), dma(blocks * p), dma(blocks * p), dma(blocks * p), dma(p), dma(p),
        ],
        compiler_params=pltpu.CompilerParams(
            collective_id=0, has_side_effects=True, vmem_limit_bytes=56 * 2**20,
            dimension_semantics=("arbitrary",),
        ),
        cost_estimate=pl.CostEstimate(
            flops=2 * rows * cols * CZ * (3 * hidden + heads + CZ),
            bytes_accessed=2 * rows * cols * (CZ + 2 * heads),
            transcendentals=rows * cols * hidden,
        ),
        name="diffusion_block",
    )(*operands)
    return single_out.T, atoms_out


def solution(mesh):
    in_specs = (
        P(("row", "col"), None),
        P(("row", "col"), None, None, None),
        P(("row", "col")),
        P("row", None),
        P("row", "col", None),
        P(),
        P(),
        P(),
        P(),
        P(),
        P(),
        P(),
        P(None, None, "col"),
        P("col", None),
        P("col", None),
    )
    out_specs = (P("row", "col"), P(("row", "col"), None))
    return jax.shard_map(body, mesh=mesh, in_specs=in_specs, out_specs=out_specs, check_vma=False)
```
